32 devices in a mesh: groups: 2 (over x), ep: 4 (over y, core), sub: 4 (over z).
Axes of the slice: x: 2, y: 2, z: 4, core: 2. Of those that a mesh axis runs over, the one named last changes fastest.
Arguments:
- tokens: bfloat16 [256, 7168], P(('groups', 'ep', 'sub')), parts along dimension 0, may hold values from -6 to 6
- routes: int32 [256, 2], P(('groups', 'ep', 'sub')), parts along dimension 0, may hold values from 0 to 3, all different within a row; in each aligned block of 8 rows (0 to 7, 8 to 15, ...) at most 4 rows name the same one
- gates: float32 [256, 2], P(('groups', 'ep', 'sub')), parts along dimension 0, may hold values from 0.05 to 1
- gate_weight: bfloat16 [4, 7168, 2048], P('ep', None, 'sub'), may hold values from -0.0625 to 0.0625
- up_weight: bfloat16 [4, 7168, 2048], P('ep', None, 'sub'), may hold values from -0.0625 to 0.0625
- down_weight: bfloat16 [4, 2048, 7168], P('ep', None, 'sub'), may hold values from -0.125 to 0.125
Outputs:
- combined: bfloat16 [256, 7168], P(('groups', 'ep', 'sub')), parts along dimension 0
The draws below stay inside these ranges and needn't reach their ends.
There are 2 independent parts, one for each index of `groups`. The reference program is written for one: setup_inputs(seed, part) draws one part's arguments, and reference() takes and returns one part's arrays. A program takes and returns all parts, laid end to end along the dimension named above; an argument that names none is the same for every part. Nothing has to cross between parts.
Inputs may be any that keep to these rules, and one draw needn't show every extreme that they name: `routes`: each token names 2 different experts. Among the tokens of one device (aligned blocks of 8 rows) no expert is named more than 4 times, and in every draw some expert is named exactly 4 times in some such block.
All inputs are finite; a program needn't handle non-finite values.
Results may differ from the reference program's by a relative error of at most 0.0058.
Values may be sent and summed in bfloat16 or wider, within the bound.
No kernel may reach another device: no remote copies, remote signals or barrier semaphores. Data moves between devices by JAX's collectives and lax.ppermute only.
A program may use at most 128 MiB of HBM per device.

```python
import math
import jax
import jax.numpy as jnp
import numpy as np
from jax import lax

D = 7168
FF = 2048
TOK_DEV = 8
EXPERTS = 4
TOP = 2
CAP = 4
TOKENS = 128
N_EP = 4
N_SUB = 4


def level_of(own_key, extent, pieces, least, top_value):
    gain, own = 1.0, jax.random.fold_in(own_key, 6)
    for axis_at, parts in pieces:
        steps = jnp.exp(jax.random.uniform(jax.random.fold_in(own, axis_at), (parts,), jnp.float32, least / len(pieces), top_value / len(pieces)))
        gain = gain * jnp.repeat(steps, extent[axis_at] // parts).reshape([-1 if axis == axis_at else 1 for axis in range(len(extent))])
    return gain


def routed_block(rng, own, number, rows, amount, top, limit, skew):
    order = jax.random.permutation(rng, amount)
    heavy_load, usual = load_shares(amount, rows * top, limit, skew, True), load_shares(amount, rows * top, limit, skew, False)
    places = jnp.arange(amount)

    def named(tallies, turn):
        used = int((tallies > 0).sum())
        fixed = max(1, used // 4)
        shifted = fixed + (places - fixed + turn * (used - fixed)) % max(1, amount - fixed)
        return jnp.zeros((amount,), jnp.int32).at[order[jnp.where(places < fixed, places, shifted)]].set(jnp.asarray(tallies, jnp.int32))

    tallies = jnp.where(number % 4 == 0, named(heavy_load, number // 4), named(usual, number - number // 4 - 1))
    mixed = jax.random.permutation(jax.random.fold_in(own, 3), amount)
    source_of, receiver = mixed[0:amount // 2 * 2:2], mixed[1:amount // 2 * 2:2]
    room = jnp.minimum(tallies[source_of] - 1, limit - tallies[receiver]) // 2
    room = jnp.where((source_of == order[0]) | (receiver == order[0]) | (tallies[receiver] == 0), 0, jnp.maximum(room, 0))
    shifted = jax.random.randint(jax.random.fold_in(own, 4), (amount // 2,), 0, 1 << 20) % (room + 1)
    tallies = tallies.at[source_of].add(-shifted).at[receiver].add(shifted)
    members = jnp.searchsorted(jnp.cumsum(tallies), jnp.arange(rows * top), side="right").astype(jnp.int32)
    grid = members.reshape(top, rows).T
    grid = grid[jax.random.permutation(jax.random.fold_in(own, 1), rows)]
    turn = jax.random.randint(jax.random.fold_in(own, 2), (rows, 1), 0, top)
    return jnp.take_along_axis(grid, (jnp.arange(top)[None, :] + turn) % top, axis=1)


def load_shares(number_of, total, bound, lean, full):
    portions = [(1 << 20) // math.isqrt(rank ** lean) + 1 for rank in range(1, number_of + 1)]
    largest = bound if full else min(bound, max(-(-total // number_of), total * portions[0] // sum(portions)))
    least = 1 if total - largest >= number_of - 1 else 0
    holding, surplus = [largest] + [least] * (number_of - 1), total - largest - least * (number_of - 1)
    while surplus > 0:
        free = [i for i in range(1, number_of) if holding[i] < largest] or [i for i in range(1, number_of) if holding[i] < bound]
        pool, left = sum([portions[i] for i in free]), surplus
        for i in free:
            addition = min(bound - holding[i], max(1, left * portions[i] // pool), surplus)
            holding[i] = holding[i] + addition
            surplus = surplus - addition
    return np.array(holding)


def centred(key, shape, width, bound, split=(), held_as=jnp.bfloat16):
    level = level_of(key, shape, split, -0.22, 0.18) if split else 1.0
    drawn = jax.random.normal(key, shape, jnp.float32) * width * level
    return jnp.minimum(jnp.maximum(drawn, -bound), bound).astype(held_as)


def setup_inputs(seed: int = 0, part: int = 0) -> dict:
    splits = jax.random.split(jax.random.key(seed), 7)
    own_keys = jax.random.split(jax.random.fold_in(splits[6], part), 7)
    tokens = centred(own_keys[0], (TOKENS, D), 1.0, 6.0, ((0, 16),))
    routes_keys = jax.random.split(jax.random.fold_in(own_keys[1], 1), TOKENS // TOK_DEV)
    routes_turns = jax.random.permutation(jax.random.fold_in(own_keys[1], 3), TOKENS // TOK_DEV)
    routes = jax.vmap(lambda own, number: routed_block(jax.random.fold_in(own_keys[1], 2), own, number, TOK_DEV, EXPERTS, TOP, CAP, 2))(routes_keys, routes_turns).reshape((TOKENS, TOP))
    gates = jnp.clip(jnp.exp(math.log(1.0) - 2.9957323 * jax.random.uniform(own_keys[2], (TOKENS, TOP), jnp.float32) ** level_of(own_keys[2], (TOKENS, TOP), ((0, 16),), -0.2, 0.2)), 0.05, 1.0)
    gate_weight = centred(splits[3], (EXPERTS, D, FF), D ** -0.5, 0.0625, ((0, 4), (2, 4)))
    up_weight = centred(splits[4], (EXPERTS, D, FF), D ** -0.5, 0.0625, ((0, 4), (2, 4)))
    down_weight = centred(splits[5], (EXPERTS, FF, D), FF ** -0.5, 0.125, ((0, 4), (2, 4)))
    return {"tokens": tokens, "routes": routes, "gates": gates, "gate_weight": gate_weight, "up_weight": up_weight, "down_weight": down_weight}


def slot_numbers(routes, owners):
    choose = (routes[:, :, None] == jnp.arange(EXPERTS, dtype=jnp.int32)[None, None, :]).astype(jnp.int32)
    present = jnp.sum(choose, axis=1).reshape(owners, TOK_DEV, EXPERTS)
    before = (jnp.cumsum(present, axis=1) - present).reshape(owners * TOK_DEV, EXPERTS)
    return jnp.sum(choose * before[:, None, :], axis=2).astype(jnp.int32)


def reference(tokens, routes, gates, gate_weight, up_weight, down_weight):
    owners = N_EP * N_SUB
    slots = slot_numbers(routes, owners)
    owner = (jnp.arange(TOKENS, dtype=jnp.int32) // TOK_DEV)[:, None]
    position = (owner * CAP + slots).astype(jnp.int32)
    token_ids = jnp.broadcast_to(jnp.arange(TOKENS, dtype=jnp.int32)[:, None], routes.shape)
    table = jnp.full((EXPERTS, owners * CAP), TOKENS, jnp.int32)
    table = table.at[routes, position].set(token_ids)
    padded = jnp.concatenate([tokens, jnp.zeros((1, D), jnp.bfloat16)], axis=0)

    def expert(operands):
        index, w_gate, w_up, w_down = operands
        rows = padded[index]
        gate = jnp.dot(rows, w_gate, preferred_element_type=jnp.float32)
        up = jnp.dot(rows, w_up, preferred_element_type=jnp.float32)
        hidden = (jax.nn.silu(gate) * up).astype(jnp.bfloat16)
        return jnp.dot(hidden, w_down, preferred_element_type=jnp.float32).astype(jnp.bfloat16)

    outputs = lax.map(expert, (table, gate_weight, up_weight, down_weight))
    picked = outputs[routes, position]
    combined = jnp.sum(gates[:, :, None] * picked.astype(jnp.float32), axis=1)
    return combined.astype(jnp.bfloat16)
```

```python
import functools

import jax
import jax.numpy as jnp
from jax import lax
from jax.experimental import pallas as pl
from jax.experimental.pallas import tpu as pltpu
from jax.sharding import PartitionSpec as P

LANES = 128


def swap(x, axis, size, k):
    return lax.ppermute(x, axis, [(i, i ^ k) for i in range(size)])


def pack_kernel(tokens, routes, out):
    count, width = tokens.shape
    chosen = routes.shape[0]
    out[:, :width] = tokens[...]
    diagonal = lax.broadcasted_iota(jnp.int32, (count, count), 0) == lax.broadcasted_iota(
        jnp.int32, (count, count), 1
    )
    lane = lax.broadcasted_iota(jnp.int32, (count, LANES), 1)
    meta = jnp.zeros((count, LANES), jnp.float32)
    for k in range(chosen):
        named = jnp.broadcast_to(routes[k:k + 1, :], (count, count)).astype(jnp.float32)
        named = jnp.sum(jnp.where(diagonal, named, 0.0), axis=1, keepdims=True)
        meta = jnp.where(lane == k, named, meta)
    out[:, width:] = meta.astype(jnp.bfloat16)


def up_kernel(count, chosen, cap, chunk, width, where, *refs):
    n = (len(refs) - 4)
    blocks, (w_gate, w_up, out, xs) = refs[:n], refs[n:]
    columns = out.shape[1]
    rows = count * chunk
    slots = cap * chunk
    expert, me = where[0], where[1]
    for b in range(0, n, 2):
        pair = jnp.concatenate([blocks[b][...], blocks[b + 1][...]], axis=0)
        xs[b * count:(b + 2) * count, :] = pair
    step = min(256, columns)

    def part(j, carry):
        at = pl.multiple_of(j * rows, rows)
        meta = jnp.transpose(xs[pl.ds(at, rows), width:width + LANES].astype(jnp.float32))
        row = lax.broadcasted_iota(jnp.int32, (LANES, rows), 0)
        named = (row < chosen) & (meta == expert.astype(jnp.float32))
        present = jnp.max(named.astype(jnp.float32), axis=0, keepdims=True)
        a = lax.broadcasted_iota(jnp.int32, (rows, rows), 0)
        b = lax.broadcasted_iota(jnp.int32, (rows, rows), 1)
        earlier = ((a // count == b // count) & (a < b)).astype(jnp.float32).astype(jnp.bfloat16)
        many = jnp.broadcast_to(present, (slots, rows))
        rank = jnp.dot(many.astype(jnp.bfloat16), earlier, preferred_element_type=jnp.float32)
        slot = lax.broadcasted_iota(jnp.int32, (slots, rows), 0)
        token = lax.broadcasted_iota(jnp.int32, (slots, rows), 1)
        owner = (token // count) ^ (me % chunk)
        pick = (slot // cap == owner) & ((slot % cap).astype(jnp.float32) == rank) & (many > 0.5)
        pick = pick.astype(jnp.float32).astype(jnp.bfloat16)
        to = pl.multiple_of((j ^ (me // chunk)) * slots, slots)
        for c in range(0, columns, step):
            x = xs[pl.ds(at, rows), :width]
            gate = jnp.dot(x, w_gate[0, :, c:c + step], preferred_element_type=jnp.float32)
            up = jnp.dot(x, w_up[0, :, c:c + step], preferred_element_type=jnp.float32)
            hidden = (gate / (1.0 + jnp.exp(-gate)) * up).astype(jnp.bfloat16)
            chosen_rows = jnp.dot(pick, hidden, preferred_element_type=jnp.float32)
            out[pl.ds(to, slots), c:c + step] = chosen_rows.astype(jnp.bfloat16)
        return carry

    lax.fori_loop(0, n // chunk, part, 0)


def down_kernel(where, *refs):
    n = len(refs) - 2
    parts, w_down, out = refs[:n], refs[n], refs[n + 1]
    depth = parts[0].shape[1]
    rows, columns = out.shape
    sub = where[0]
    step = 256 if columns % 256 == 0 else 128
    rstep = min(rows, 128)

    def part(j, carry):
        at = pl.multiple_of(j * rstep, rstep)
        for c in range(0, columns, step):
            total = None
            for k in range(n):
                d = pl.multiple_of((sub ^ k) * depth, depth)
                term = jnp.dot(
                    parts[k][pl.ds(at, rstep), :],
                    w_down[0, pl.ds(d, depth), c:c + step],
                    preferred_element_type=jnp.float32,
                )
                total = term if total is None else total + term
            out[pl.ds(at, rstep), c:c + step] = total.astype(jnp.bfloat16)
        return carry

    lax.fori_loop(0, rows // rstep, part, 0)


def body(tokens, routes, gates, gate_weight, up_weight, down_weight):
    experts = lax.axis_size("ep")
    groups = lax.axis_size("sub")
    ep, sub = lax.axis_index("ep"), lax.axis_index("sub")
    count, width = tokens.shape
    chosen = routes.shape[1]
    slot_cap = count * chosen * 9 // (8 * experts)
    devices = experts * groups

    vmem = pl.BlockSpec(memory_space=pltpu.VMEM)
    smem = pl.BlockSpec(memory_space=pltpu.SMEM)
    own = pl.pallas_call(
        pack_kernel,
        out_shape=jax.ShapeDtypeStruct((count, width + LANES), jnp.bfloat16),
        in_specs=[vmem, vmem],
        out_specs=vmem,
        cost_estimate=pl.CostEstimate(flops=20 * 10**9, bytes_accessed=0, transcendentals=0),
        compiler_params=pltpu.CompilerParams(vmem_limit_bytes=1 << 20),
        name="pack",
    )(tokens, routes.T)
    got = {(0, 0): own}
    for kz in sorted(range(1, groups), reverse=True):
        got[kz, 0] = swap(own, "sub", groups, kz)
    for kz in range(groups):
        for ky in range(2, experts, 2):
            got[kz, ky] = swap(got[kz, 0], "ep", experts, ky)
    for kz in range(groups):
        for ky in range(0, experts, 2):
            got[kz, ky + 1] = swap(got[kz, ky], "ep", experts, 1)
    blocks = [got[kz, ke] for ke in range(experts) for kz in range(groups)]

    columns = gate_weight.shape[2]
    chunk = min(16, devices)
    where = jnp.stack([ep, ep * groups + sub]).astype(jnp.int32)
    hidden = pl.pallas_call(
        functools.partial(up_kernel, count, chosen, slot_cap, chunk, width),
        out_shape=jax.ShapeDtypeStruct((devices * slot_cap, columns), jnp.bfloat16),
        in_specs=[smem] + [vmem] * (devices + 2),
        out_specs=vmem,
        scratch_shapes=[pltpu.VMEM((devices * count, width + LANES), jnp.bfloat16)],
        compiler_params=pltpu.CompilerParams(vmem_limit_bytes=(20 << 20) * (1 if devices <= 16 else 2)),
        name="gate_up",
    )(where, *blocks, gate_weight, up_weight)

    parts = [hidden] + [swap(hidden, "sub", groups, k) for k in range(1, groups)]
    out_cols = down_weight.shape[2]
    result = pl.pallas_call(
        down_kernel,
        out_shape=jax.ShapeDtypeStruct((devices * slot_cap, out_cols), jnp.bfloat16),
        in_specs=[smem] + [vmem] * (groups + 1),
        out_specs=vmem,
        compiler_params=pltpu.CompilerParams(vmem_limit_bytes=16 << 20),
        name="down",
    )(sub[None].astype(jnp.int32), *parts, down_weight)

    choose = (routes[:, :, None] == jnp.arange(experts, dtype=jnp.int32)[None, None, :]).astype(jnp.int32)
    present = jnp.sum(choose, axis=1)
    before = jnp.cumsum(present, axis=0) - present
    slots = jnp.sum(choose * before[:, None, :], axis=2)
    target = routes * slot_cap + slots
    select = (
        target[:, :, None] == jnp.arange(experts * slot_cap, dtype=jnp.int32)[None, None, :]
    ).astype(jnp.float32)
    weighting = jnp.sum(select * gates[:, :, None], axis=1).reshape(count, experts, slot_cap)
    returned = lax.all_to_all(
        result.reshape(devices, slot_cap, out_cols),
        ("ep", "sub"),
        split_axis=0,
        concat_axis=2,
        tiled=True,
    )
    returned = returned.reshape(slot_cap, experts, width).astype(jnp.float32)
    combined = jnp.einsum("tec,ced->td", weighting, returned, precision=lax.Precision.HIGHEST)
    return combined.astype(jnp.bfloat16)


def solution(mesh):
    return jax.shard_map(
        body,
        mesh=mesh,
        in_specs=(
            P(("groups", "ep", "sub"), None),
            P(("groups", "ep", "sub"), None),
            P(("groups", "ep", "sub"), None),
            P("ep", None, "sub"),
            P("ep", None, "sub"),
            P("ep", None, "sub"),
        ),
        out_specs=P(("groups", "ep", "sub"), None),
        check_vma=False,
    )
```

```python
import functools

import jax
import jax.numpy as jnp
from jax import lax
from jax.experimental import pallas as pl
from jax.experimental.pallas import tpu as pltpu
from jax.sharding import PartitionSpec as P

LANES = 128
PIECES = 3
VMEM = pl.BlockSpec(memory_space=pltpu.VMEM)
HBM = pl.BlockSpec(memory_space=pltpu.HBM)


def iota(shape, dim):
    return lax.broadcasted_iota(jnp.int32, shape, dim)


def as_bf16(mask):
    return mask.astype(jnp.float32).astype(jnp.bfloat16)


def swap(x, axis, size, k):
    return lax.ppermute(x, axis, [(i, i ^ k) for i in range(size)])


def pack_kernel(tokens, routes, gates, out, named, shares, sems):
    count, width = tokens.shape
    chosen = routes.shape[0]
    moves = [
        pltpu.make_async_copy(routes, named, sems.at[0]),
        pltpu.make_async_copy(gates, shares, sems.at[1]),
        pltpu.make_async_copy(tokens, out.at[:, pl.ds(0, width)], sems.at[2]),
    ]
    for move in moves:
        move.start()
    for move in moves[:2]:
        move.wait()
    diagonal = iota((count, count), 0) == iota((count, count), 1)
    lane = iota((count, LANES), 1)
    meta = jnp.zeros((count, LANES), jnp.float32)
    for k in range(chosen):
        columns = [named[k:k + 1, :].astype(jnp.float32)]
        rest = shares[k:k + 1, :]
        for _ in range(PIECES):
            piece = rest.astype(jnp.bfloat16).astype(jnp.float32)
            columns.append(piece)
            rest = rest - piece
        for p, value in enumerate(columns):
            value = jnp.where(diagonal, jnp.broadcast_to(value, (count, count)), 0.0)
            meta = jnp.where(lane == p * chosen + k, jnp.sum(value, axis=1, keepdims=True), meta)
    out[:, width:] = meta.astype(jnp.bfloat16)
    moves[2].wait()


def up_kernel(count, chosen, cap, chunk, width, *refs):
    n = len(refs) - 4
    blocks, (w_gate, w_up, out, xs) = refs[:n], refs[n:]
    columns = out.shape[1]
    rows = count * chunk
    slots = cap * chunk
    expert = lax.axis_index("ep")
    me = expert * lax.axis_size("sub") + lax.axis_index("sub")
    for b in range(0, n, 2):
        pair = jnp.concatenate([blocks[b][...], blocks[b + 1][...]], axis=0)
        xs[b * count:(b + 2) * count, :] = pair
    step = min(256, columns)

    def part(j, carry):
        at = pl.multiple_of(j * rows, rows)
        meta = jnp.transpose(xs[pl.ds(at, rows), width:width + LANES].astype(jnp.float32))
        named = (iota((LANES, rows), 0) < chosen) & (meta == expert.astype(jnp.float32))
        present = jnp.max(named.astype(jnp.float32), axis=0, keepdims=True)
        a, b = iota((rows, rows), 0), iota((rows, rows), 1)
        earlier = as_bf16((a // count == b // count) & (a < b))
        many = jnp.broadcast_to(present, (slots, rows))
        rank = jnp.dot(many.astype(jnp.bfloat16), earlier, preferred_element_type=jnp.float32)
        slot, token = iota((slots, rows), 0), iota((slots, rows), 1)
        owner = (token // count) ^ (me % chunk)
        pick = (slot // cap == owner) & ((slot % cap).astype(jnp.float32) == rank) & (many > 0.5)
        pick = as_bf16(pick)
        to = pl.multiple_of((j ^ (me // chunk)) * slots, slots)
        for c in range(0, columns, step):
            x = xs[pl.ds(at, rows), :width]
            gate = jnp.dot(x, w_gate[0, :, c:c + step], preferred_element_type=jnp.float32)
            up = jnp.dot(x, w_up[0, :, c:c + step], preferred_element_type=jnp.float32)
            hidden = (gate / (1.0 + jnp.exp(-gate)) * up).astype(jnp.bfloat16)
            picked = jnp.dot(pick, hidden, preferred_element_type=jnp.float32)
            out[pl.ds(to, slots), c:c + step] = picked.astype(jnp.bfloat16)
        return carry

    lax.fori_loop(0, n // chunk, part, 0)


def down_kernel(experts, groups, *refs):
    parts, w_down = refs[:groups], refs[groups]
    outs, rows = refs[groups + 1:groups + 1 + experts], refs[-1]
    depth = parts[0].shape[1]
    each, columns = outs[0].shape
    ep, sub = lax.axis_index("ep"), lax.axis_index("sub")
    for e in range(experts):
        at = pl.multiple_of((ep ^ e) * each, each)
        for k in range(groups):
            rows[e * each:(e + 1) * each, k * depth:(k + 1) * depth] = parts[k][pl.ds(at, each), :]
    step = 256 if columns % 256 == 0 else 128
    for c in range(0, columns, step):
        total = None
        for k in range(groups):
            d = pl.multiple_of((sub ^ k) * depth, depth)
            term = jnp.dot(
                rows[:, k * depth:(k + 1) * depth],
                w_down[0, pl.ds(d, depth), c:c + step],
                preferred_element_type=jnp.float32,
            )
            total = term if total is None else total + term
        total = total.astype(jnp.bfloat16)
        for e in range(experts):
            outs[e][:, c:c + step] = total[e * each:(e + 1) * each, :]


def combine_kernel(experts, groups, count, chosen, cap, width, *refs):
    blocks, got = refs[:groups], refs[groups:groups + experts]
    outs, rows = refs[groups + experts:-1], refs[-1]
    each = got[0].shape[0]
    tokens = groups * count
    ep, sub = lax.axis_index("ep"), lax.axis_index("sub")
    for e in range(experts):
        rows[e * each:(e + 1) * each, :] = got[e][...]
    meta = jnp.concatenate([b[:, width:width + LANES].astype(jnp.float32) for b in blocks], axis=0)
    a, b = iota((tokens, tokens), 0), iota((tokens, tokens), 1)
    earlier = as_bf16((a // count == b // count) & (b < a))
    lane = iota((tokens, LANES), 1)
    token, slot = iota((tokens, each), 0), iota((tokens, each), 1)
    mine = slot // cap == (token // count) ^ sub
    place = (slot % cap).astype(jnp.float32)
    weights = [[] for _ in range(PIECES)]
    for e in range(experts):
        named = ((lane < chosen) & (meta == (ep ^ e).astype(jnp.float32))).astype(jnp.float32)
        present = jnp.broadcast_to(jnp.max(named, axis=1, keepdims=True), (tokens, each))
        rank = jnp.dot(earlier, present.astype(jnp.bfloat16), preferred_element_type=jnp.float32)
        taken = mine & (place == rank) & (present > 0.5)
        for p in range(PIECES):
            share = 0.0
            for k in range(chosen):
                at = (p + 1) * chosen + k
                share = share + meta[:, at:at + 1] * named[:, k:k + 1]
            weights[p].append(jnp.where(taken, share, 0.0))
    weights = [jnp.concatenate(w, axis=1).astype(jnp.bfloat16) for w in weights]
    total = 0.0
    for w in weights[::-1]:
        total = total + jnp.dot(w, rows[...], preferred_element_type=jnp.float32)
    total = total.astype(jnp.bfloat16)
    for k in range(groups):
        outs[k][...] = total[k * count:(k + 1) * count, :]


def place_kernel(*refs):
    parts, out, sems = refs[:-2], refs[-2], refs[-1]
    columns = parts[0].shape[1]
    sub = lax.axis_index("sub")
    moves = []
    for k, part in enumerate(parts):
        at = pl.multiple_of((sub ^ k) * columns, columns)
        moves.append(pltpu.make_async_copy(part, out.at[:, pl.ds(at, columns)], sems.at[k]))
    for move in moves:
        move.start()
    for move in moves:
        move.wait()


def body(tokens, routes, gates, gate_weight, up_weight, down_weight):
    experts = lax.axis_size("ep")
    groups = lax.axis_size("sub")
    count, width = tokens.shape
    chosen = routes.shape[1]
    cap = count * chosen * 9 // (8 * experts)
    devices = experts * groups
    chunk = min(16, devices)

    def array(*shape):
        return jax.ShapeDtypeStruct(shape, jnp.bfloat16)

    def limit(mib):
        return pltpu.CompilerParams(vmem_limit_bytes=mib << 20)

    own = pl.pallas_call(
        pack_kernel,
        out_shape=array(count, width + LANES),
        in_specs=[HBM, HBM, HBM],
        out_specs=VMEM,
        scratch_shapes=[
            pltpu.VMEM((chosen, count), jnp.int32),
            pltpu.VMEM((chosen, count), jnp.float32),
            pltpu.SemaphoreType.DMA((3,)),
        ],
        compiler_params=limit(1),
        cost_estimate=pl.CostEstimate(flops=20000000000, bytes_accessed=0, transcendentals=0),
        name="pack",
    )(tokens, routes.T, gates.T)

    got = {(0, 0): own}
    single = [1 << b for b in range(groups.bit_length() - 1)]
    far = range(2, experts, 2)
    for kz in single[::-1]:
        got[kz, 0] = swap(own, "sub", groups, kz)
    for ky in far:
        got[0, ky] = swap(own, "ep", experts, ky)
    relayed = [kz for kz in range(1, groups) if kz not in single]
    for kz in relayed:
        for ky in far:
            got[kz, ky] = swap(got[0, ky], "sub", groups, kz)
    for kz in relayed:
        low = kz & -kz
        got[kz, 0] = swap(got[kz ^ low, 0], "sub", groups, low)
    for kz in single:
        for ky in far:
            got[kz, ky] = swap(got[kz, 0], "ep", experts, ky)
    for kz in range(groups):
        for ky in range(0, experts, 2):
            got[kz, ky + 1] = swap(got[kz, ky], "ep", experts, 1)
    blocks = [got[kz, ke] for ke in range(experts) for kz in range(groups)]

    columns = gate_weight.shape[2]
    hidden = pl.pallas_call(
        functools.partial(up_kernel, count, chosen, cap, chunk, width),
        out_shape=array(devices * cap, columns),
        in_specs=[VMEM] * (devices + 2),
        out_specs=VMEM,
        scratch_shapes=[pltpu.VMEM((devices * count, width + LANES), jnp.bfloat16)],
        compiler_params=limit(12 if devices <= 16 else 24),
        name="gate_up",
    )(*blocks, gate_weight, up_weight)

    parts = [hidden] + [swap(hidden, "sub", groups, k) for k in range(1, groups)]
    out_cols = down_weight.shape[2]
    sent = pl.pallas_call(
        functools.partial(down_kernel, experts, groups),
        out_shape=[array(groups * cap, out_cols)] * experts,
        in_specs=[VMEM] * (groups + 1),
        out_specs=[VMEM] * experts,
        scratch_shapes=[pltpu.VMEM((devices * cap, groups * columns), jnp.bfloat16)],
        compiler_params=limit(8 if devices <= 16 else 24),
        name="down",
    )(*parts, down_weight)

    came = [sent[0]] + [swap(sent[e], "ep", experts, e) for e in range(1, experts)]
    summed = pl.pallas_call(
        functools.partial(combine_kernel, experts, groups, count, chosen, cap, width),
        out_shape=[array(count, out_cols)] * groups,
        in_specs=[VMEM] * (groups + experts),
        out_specs=[VMEM] * groups,
        scratch_shapes=[pltpu.VMEM((devices * cap, out_cols), jnp.bfloat16)],
        compiler_params=limit(8 if devices <= 16 else 24),
        name="combine",
    )(*[got[k, 0] for k in range(groups)], *came)

    home = [summed[0]] + [swap(summed[k], "sub", groups, k) for k in range(1, groups)]
    return pl.pallas_call(
        place_kernel,
        out_shape=array(count, width),
        in_specs=[VMEM] * groups,
        out_specs=HBM,
        scratch_shapes=[pltpu.SemaphoreType.DMA((groups,))],
        compiler_params=limit(1),
        name="place",
    )(*home)


def solution(mesh):
    return jax.shard_map(
        body,
        mesh=mesh,
        in_specs=(
            P(("groups", "ep", "sub"), None),
            P(("groups", "ep", "sub"), None),
            P(("groups", "ep", "sub"), None),
            P("ep", None, "sub"),
            P("ep", None, "sub"),
            P("ep", None, "sub"),
        ),
        out_specs=P(("groups", "ep", "sub"), None),
        check_vma=False,
    )
```

```python
import functools

import jax
import jax.numpy as jnp
from jax import lax
from jax.experimental import pallas as pl
from jax.experimental.pallas import tpu as pltpu
from jax.sharding import PartitionSpec as P

LANES = 128
PIECES = 3
VMEM = pl.BlockSpec(memory_space=pltpu.VMEM)
HBM = pl.BlockSpec(memory_space=pltpu.HBM)


def iota(shape, dim):
    return lax.broadcasted_iota(jnp.int32, shape, dim)


def as_bf16(mask):
    return mask.astype(jnp.float32).astype(jnp.bfloat16)


def swap(x, axis, size, k):
    return lax.ppermute(x, axis, [(i, i ^ k) for i in range(size)])


def pack_kernel(tokens, routes, gates, out, named, shares, sems):
    count, width = tokens.shape
    chosen = routes.shape[0]
    moves = [
        pltpu.make_async_copy(routes, named, sems.at[0]),
        pltpu.make_async_copy(gates, shares, sems.at[1]),
        pltpu.make_async_copy(tokens, out.at[:, pl.ds(0, width)], sems.at[2]),
    ]
    for move in moves[:3]:
        move.start()
    for move in moves[:2]:
        move.wait()
    diagonal = iota((count, count), 0) == iota((count, count), 1)
    lane = iota((count, LANES), 1)
    me = lax.axis_index("ep") * lax.axis_size("sub") + lax.axis_index("sub")
    owner = (PIECES + 1) * chosen
    meta = jnp.where(lane == owner, me.astype(jnp.float32), jnp.zeros((count, LANES), jnp.float32))
    for k in range(chosen):
        columns = [named[k:k + 1, :].astype(jnp.float32)]
        rest = shares[k:k + 1, :]
        for _ in range(PIECES):
            piece = rest.astype(jnp.bfloat16).astype(jnp.float32)
            columns.append(piece)
            rest = rest - piece
        for p, value in enumerate(columns):
            value = jnp.where(diagonal, jnp.broadcast_to(value, (count, count)), 0.0)
            meta = jnp.where(lane == p * chosen + k, jnp.sum(value, axis=1, keepdims=True), meta)
    out[:, width:] = meta.astype(jnp.bfloat16)
    moves[2].wait()


def gather_rows(arrays, xs):
    at, held = 0, None
    for ref in arrays:
        rows = ref.shape[0]
        if rows % 16 == 0:
            xs[at:at + rows, :] = ref[...]
            at += rows
        elif held is None:
            held = ref
        else:
            xs[at:at + 2 * rows, :] = jnp.concatenate([held[...], ref[...]], axis=0)
            at, held = at + 2 * rows, None


def hold_kernel(x, out):
    out[...] = x[...]


def up_kernel(n, count, chosen, cap, chunk, width, *refs):
    arrays, (w_gate, w_up, out, xs, total) = refs[:n], refs[n:]
    columns = out.shape[1]
    slots = out.shape[0]
    rows = count * chunk
    parts = xs.shape[0] // rows
    expert = lax.axis_index("ep")
    gather_rows(arrays, xs)
    step = min(256, columns)

    def part(j, carry):
        at = pl.multiple_of(j * rows, rows)
        meta = jnp.transpose(xs[pl.ds(at, rows), width:width + LANES].astype(jnp.float32))
        named = (iota((LANES, rows), 0) < chosen) & (meta == expert.astype(jnp.float32))
        present = jnp.max(named.astype(jnp.float32), axis=0, keepdims=True)
        a, b = iota((rows, rows), 0), iota((rows, rows), 1)
        earlier = as_bf16((a // count == b // count) & (a < b))
        many = jnp.broadcast_to(present, (slots, rows))
        rank = jnp.dot(many.astype(jnp.bfloat16), earlier, preferred_element_type=jnp.float32)
        slot = iota((slots, rows), 0)
        lane = (PIECES + 1) * chosen
        mine = (slot // cap).astype(jnp.float32) == meta[lane:lane + 1, :]
        pick = as_bf16(mine & ((slot % cap).astype(jnp.float32) == rank) & (many > 0.5))
        for c in range(0, columns, step):
            x = xs[pl.ds(at, rows), :width]
            gate = jnp.dot(x, w_gate[0, :, c:c + step], preferred_element_type=jnp.float32)
            up = jnp.dot(x, w_up[0, :, c:c + step], preferred_element_type=jnp.float32)
            hidden = (gate / (1.0 + jnp.exp(-gate)) * up).astype(jnp.bfloat16)
            picked = jnp.dot(pick, hidden, preferred_element_type=jnp.float32)
            if parts == 1:
                out[:, c:c + step] = picked.astype(jnp.bfloat16)
            else:
                total[:, c:c + step] += picked
        return carry

    if parts == 1:
        part(0, 0)
    else:
        total[...] = jnp.zeros_like(total)
        lax.fori_loop(0, parts, part, 0)
        out[...] = total[...].astype(jnp.bfloat16)


def down_kernel(experts, first, n, last, *refs):
    parts, w_down = refs[:n][::-1], refs[n]
    before = None if first == 0 else refs[n + 1]
    outs, rows = refs[n + 1 + (first > 0):-1], refs[-1]
    count, depth = parts[0].shape
    columns = w_down.shape[2]
    each = count // experts
    ep, sub = lax.axis_index("ep"), lax.axis_index("sub")
    for e in range(experts):
        at = pl.multiple_of((ep ^ e) * each, each)
        for k in range(n):
            rows[e * each:(e + 1) * each, k * depth:(k + 1) * depth] = parts[k][pl.ds(at, each), :]
    step = 256 if columns % 256 == 0 else 128
    for c in range(0, columns, step):
        total = None if before is None else before[:, c:c + step]
        for k in range(n):
            d = pl.multiple_of((sub ^ (first + k)) * depth, depth)
            term = jnp.dot(
                rows[:, k * depth:(k + 1) * depth],
                w_down[0, pl.ds(d, depth), c:c + step],
                preferred_element_type=jnp.float32,
            )
            total = term if total is None else total + term
        if not last:
            outs[0][:, c:c + step] = total
            continue
        total = total.astype(jnp.bfloat16)
        for e in range(experts):
            outs[e][:, c:c + step] = total[e * each:(e + 1) * each, :]


def share_kernel(experts, groups, count, chosen, cap, width, *refs):
    blocks, outs = refs[:groups], refs[groups:]
    each = groups * cap
    tokens = groups * count
    ep, sub = lax.axis_index("ep"), lax.axis_index("sub")
    meta = jnp.concatenate([b[:, width:width + LANES].astype(jnp.float32) for b in blocks], axis=0)
    a, b = iota((tokens, tokens), 0), iota((tokens, tokens), 1)
    earlier = as_bf16((a // count == b // count) & (b < a))
    lane = iota((tokens, LANES), 1)
    token, slot = iota((tokens, each), 0), iota((tokens, each), 1)
    mine = slot // cap == (token // count) ^ sub
    place = (slot % cap).astype(jnp.float32)
    weights = [[] for _ in range(PIECES)]
    for e in range(experts):
        named = ((lane < chosen) & (meta == (ep ^ e).astype(jnp.float32))).astype(jnp.float32)
        present = jnp.broadcast_to(jnp.max(named, axis=1, keepdims=True), (tokens, each))
        rank = jnp.dot(earlier, present.astype(jnp.bfloat16), preferred_element_type=jnp.float32)
        taken = mine & (place == rank) & (present > 0.5)
        for p in range(PIECES):
            share = 0.0
            for k in range(chosen):
                at = (p + 1) * chosen + k
                share = share + meta[:, at:at + 1] * named[:, k:k + 1]
            weights[p].append(jnp.where(taken, share, 0.0))
    for p in range(PIECES):
        outs[p][...] = jnp.concatenate(weights[p], axis=1).astype(jnp.bfloat16)


def combine_kernel(experts, groups, count, *refs):
    weights, got = refs[:PIECES], refs[PIECES:PIECES + experts]
    outs, rows = refs[PIECES + experts:-1], refs[-1]
    each = got[0].shape[0]
    for e in range(experts):
        rows[e * each:(e + 1) * each, :] = got[e][...]
    total = 0.0
    for w in weights[::-1]:
        total = total + jnp.dot(w[...], rows[...], preferred_element_type=jnp.float32)
    total = total.astype(jnp.bfloat16)
    for k in range(groups):
        outs[k][...] = total[k * count:(k + 1) * count, :]


def place_kernel(*refs):
    parts, out, sems = refs[:-2][::-1], refs[-2], refs[-1]
    columns = parts[0].shape[1]
    sub = lax.axis_index("sub")
    moves = []
    for k, part in enumerate(parts):
        at = pl.multiple_of((sub ^ k) * columns, columns)
        moves.append(pltpu.make_async_copy(part, out.at[:, pl.ds(at, columns)], sems.at[k]))
    for move in moves:
        move.start()
    for move in moves:
        move.wait()


def body(tokens, routes, gates, gate_weight, up_weight, down_weight):
    experts = lax.axis_size("ep")
    groups = lax.axis_size("sub")
    count, width = tokens.shape
    chosen = routes.shape[1]
    cap = count * chosen * 9 // (8 * experts)
    devices = experts * groups
    chunk = min(16, devices)

    def array(*shape):
        return jax.ShapeDtypeStruct(shape, jnp.bfloat16)

    def limit(mib):
        return pltpu.CompilerParams(vmem_limit_bytes=mib << 20)

    own = pl.pallas_call(
        pack_kernel,
        out_shape=array(count, width + LANES),
        in_specs=[HBM] * 3,
        out_specs=VMEM,
        scratch_shapes=[
            pltpu.VMEM((chosen, count), jnp.int32),
            pltpu.VMEM((chosen, count), jnp.float32),
            pltpu.SemaphoreType.DMA((3,)),
        ],
        compiler_params=pltpu.CompilerParams(vmem_limit_bytes=67_000_000),
        name="pack",
    )(tokens, routes.T, gates.T)

    def hold(x):
        return pl.pallas_call(
            hold_kernel,
            out_shape=array(*x.shape),
            in_specs=[VMEM],
            out_specs=VMEM,
            cost_estimate=pl.CostEstimate(flops=3000000000, bytes_accessed=0, transcendentals=0),
            compiler_params=limit(1),
            name="hold",
        )(x)

    got = {(0, 0): own}
    single = [1 << b for b in range(groups.bit_length() - 1)]
    far = range(2, experts, 2)
    for kz in single[::-1]:
        got[kz, 0] = swap(own, "sub", groups, kz)
    for ky in far:
        got[0, ky] = swap(own, "ep", experts, ky)
    got[0, 2] = hold(got[0, 2])
    got[1, 0] = hold(got[1, 0])
    relayed = [kz for kz in range(1, groups) if kz not in single]
    for kz in relayed:
        for ky in far:
            got[kz, ky] = swap(got[0, ky], "sub", groups, kz)
    for kz in relayed:
        low = kz & -kz
        got[kz, 0] = swap(got[kz ^ low, 0], "sub", groups, low)
    for kz in single:
        for ky in far:
            got[kz, ky] = swap(got[kz, 0], "ep", experts, ky)
    TIE = {(0, 0): (2, 2), (1, 0): (2, 2), (2, 0): (3, 2), (0, 2): (3, 2)}
    for kz in range(groups):
        for ky in range(0, experts, 2):
            block = got[kz, ky]
            if (kz, ky) in TIE:
                block = lax.optimization_barrier((block, got[TIE[kz, ky]]))[0]
            got[kz, ky + 1] = swap(block, "ep", experts, 1)
    arrays = [got[kz, ke] for ke in range(experts) for kz in range(groups)][::-1]

    columns = gate_weight.shape[2]
    hidden = pl.pallas_call(
        functools.partial(up_kernel, len(arrays), count, chosen, cap, chunk, width),
        out_shape=array(devices * cap, columns),
        in_specs=[VMEM] * (len(arrays) + 2),
        out_specs=VMEM,
        scratch_shapes=[
            pltpu.VMEM((devices * count, width + LANES), jnp.bfloat16),
            pltpu.VMEM((devices * cap, columns), jnp.float32),
        ],
        compiler_params=limit(12 if devices <= 16 else 24),
        name="gate_up",
    )(*arrays, gate_weight, up_weight)

    parts = [hidden] + [swap(hidden, "sub", groups, k) for k in range(1, groups)]
    shares = pl.pallas_call(
        functools.partial(share_kernel, experts, groups, count, chosen, cap, width),
        out_shape=[array(groups * count, devices * cap)] * PIECES,
        in_specs=[VMEM] * groups,
        out_specs=[VMEM] * PIECES,
        compiler_params=limit(8 if devices <= 16 else 24),
        name="shares",
    )(*[got[k, 0] for k in range(groups)])
    out_cols = down_weight.shape[2]

    def down(first, n, *more):
        last = first + n == groups
        out = [array(groups * cap, out_cols)] * experts
        if not last:
            out = [jax.ShapeDtypeStruct((devices * cap, out_cols), jnp.float32)]
        return pl.pallas_call(
            functools.partial(down_kernel, experts, first, n, last),
            out_shape=out,
            in_specs=[VMEM] * (n + 1 + (first > 0)),
            out_specs=[VMEM] * len(out),
            scratch_shapes=[pltpu.VMEM((devices * cap, n * columns), jnp.bfloat16)],
            compiler_params=limit(8 if devices <= 16 else 24),
            name=f"down_{first}",
        )(*(parts[first:first + n][::-1] if first else more), down_weight, *(more if first else ()))

    own_part, *shares = lax.optimization_barrier([parts[0]] + list(shares))
    sent = down(1, groups - 1, *down(0, 1, own_part))

    came = [sent[0]] + [swap(sent[e], "ep", experts, e) for e in range(1, experts)]
    summed = pl.pallas_call(
        functools.partial(combine_kernel, experts, groups, count),
        out_shape=[array(count, out_cols)] * groups,
        in_specs=[VMEM] * (PIECES + experts),
        out_specs=[VMEM] * groups,
        scratch_shapes=[pltpu.VMEM((devices * cap, out_cols), jnp.bfloat16)],
        compiler_params=limit(8 if devices <= 16 else 24),
        name="combine",
    )(*shares, *came)

    home = [summed[0]] + [swap(summed[k], "sub", groups, k) for k in range(1, groups)]
    return pl.pallas_call(
        place_kernel,
        out_shape=array(count, width),
        in_specs=[VMEM] * groups,
        out_specs=HBM,
        scratch_shapes=[pltpu.SemaphoreType.DMA((groups,))],
        compiler_params=limit(1),
        name="place",
    )(*home[::-1])


def solution(mesh):
    return jax.shard_map(
        body,
        mesh=mesh,
        in_specs=(
            P(("groups", "ep", "sub"), None),
            P(("groups", "ep", "sub"), None),
            P(("groups", "ep", "sub"), None),
            P("ep", None, "sub"),
            P("ep", None, "sub"),
            P("ep", None, "sub"),
        ),
        out_specs=P(("groups", "ep", "sub"), None),
        check_vma=False,
    )
```

```python
import functools

import jax
import jax.numpy as jnp
from jax import lax
from jax.experimental import pallas as pl
from jax.experimental.pallas import tpu as pltpu
from jax.sharding import PartitionSpec as P

LANES = 128
PIECES = 3
VMEM = pl.BlockSpec(memory_space=pltpu.VMEM)
HBM = pl.BlockSpec(memory_space=pltpu.HBM)


def iota(shape, dim):
    return lax.broadcasted_iota(jnp.int32, shape, dim)


def as_bf16(mask):
    return mask.astype(jnp.float32).astype(jnp.bfloat16)


def swap(x, axis, size, k):
    return lax.ppermute(x, axis, [(i, i ^ k) for i in range(size)])


def pack_kernel(tokens, routes, gates, out, named, shares, sems):
    count, width = tokens.shape
    chosen = routes.shape[0]
    moves = [
        pltpu.make_async_copy(routes, named, sems.at[0]),
        pltpu.make_async_copy(gates, shares, sems.at[1]),
        pltpu.make_async_copy(tokens, out.at[:, pl.ds(0, width)], sems.at[2]),
    ]
    for move in moves[:3]:
        move.start()
    for move in moves[:2]:
        move.wait()
    diagonal = iota((count, count), 0) == iota((count, count), 1)
    lane = iota((count, LANES), 1)
    me = lax.axis_index("ep") * lax.axis_size("sub") + lax.axis_index("sub")
    owner = (PIECES + 1) * chosen
    meta = jnp.where(lane == owner, me.astype(jnp.float32), jnp.zeros((count, LANES), jnp.float32))
    for k in range(chosen):
        columns = [named[k:k + 1, :].astype(jnp.float32)]
        rest = shares[k:k + 1, :]
        for _ in range(PIECES):
            piece = rest.astype(jnp.bfloat16).astype(jnp.float32)
            columns.append(piece)
            rest = rest - piece
        for p, value in enumerate(columns):
            value = jnp.where(diagonal, jnp.broadcast_to(value, (count, count)), 0.0)
            meta = jnp.where(lane == p * chosen + k, jnp.sum(value, axis=1, keepdims=True), meta)
    out[:, width:] = meta.astype(jnp.bfloat16)
    moves[2].wait()


def gather_rows(arrays, xs):
    at, held = 0, None
    for ref in arrays:
        rows = ref.shape[0]
        if rows % 16 == 0:
            xs[at:at + rows, :] = ref[...]
            at += rows
        elif held is None:
            held = ref
        else:
            xs[at:at + 2 * rows, :] = jnp.concatenate([held[...], ref[...]], axis=0)
            at, held = at + 2 * rows, None


def hold_kernel(x, out):
    out[...] = x[...]


def up_kernel(n, count, chosen, cap, chunk, width, *refs):
    arrays, (w_gate, w_up, out, xs, total) = refs[:n], refs[n:]
    columns = out.shape[1]
    slots = out.shape[0]
    rows = count * chunk
    parts = xs.shape[0] // rows
    expert = lax.axis_index("ep")
    gather_rows(arrays, xs)
    step = min(256, columns)

    def part(j, carry):
        at = pl.multiple_of(j * rows, rows)
        meta = jnp.transpose(xs[pl.ds(at, rows), width:width + LANES].astype(jnp.float32))
        named = (iota((LANES, rows), 0) < chosen) & (meta == expert.astype(jnp.float32))
        present = jnp.max(named.astype(jnp.float32), axis=0, keepdims=True)
        a, b = iota((rows, rows), 0), iota((rows, rows), 1)
        earlier = as_bf16((a // count == b // count) & (a < b))
        many = jnp.broadcast_to(present, (slots, rows))
        rank = jnp.dot(many.astype(jnp.bfloat16), earlier, preferred_element_type=jnp.float32)
        slot = iota((slots, rows), 0)
        lane = (PIECES + 1) * chosen
        mine = (slot // cap).astype(jnp.float32) == meta[lane:lane + 1, :]
        pick = as_bf16(mine & ((slot % cap).astype(jnp.float32) == rank) & (many > 0.5))
        for c in range(0, columns, step):
            x = xs[pl.ds(at, rows), :width]
            gate = jnp.dot(x, w_gate[0, :, c:c + step], preferred_element_type=jnp.float32)
            up = jnp.dot(x, w_up[0, :, c:c + step], preferred_element_type=jnp.float32)
            hidden = (gate / (1.0 + jnp.exp(-gate)) * up).astype(jnp.bfloat16)
            picked = jnp.dot(pick, hidden, preferred_element_type=jnp.float32)
            if parts == 1:
                out[:, c:c + step] = picked.astype(jnp.bfloat16)
            else:
                total[:, c:c + step] += picked
        return carry

    if parts == 1:
        part(0, 0)
    else:
        total[...] = jnp.zeros_like(total)
        lax.fori_loop(0, parts, part, 0)
        out[...] = total[...].astype(jnp.bfloat16)


def down_kernel(experts, first, n, last, *refs):
    parts, w_down = refs[:n][::-1], refs[n]
    before = None if first == 0 else refs[n + 1]
    outs, rows = refs[n + 1 + (first > 0):-1], refs[-1]
    count, depth = parts[0].shape
    columns = w_down.shape[2]
    each = count // experts
    ep, sub = lax.axis_index("ep"), lax.axis_index("sub")
    for e in range(experts):
        at = pl.multiple_of((ep ^ e) * each, each)
        for k in range(n):
            rows[e * each:(e + 1) * each, k * depth:(k + 1) * depth] = parts[k][pl.ds(at, each), :]
    step = 256 if columns % 256 == 0 else 128
    for c in range(0, columns, step):
        total = None if before is None else before[:, c:c + step]
        for k in range(n):
            d = pl.multiple_of((sub ^ (first + k)) * depth, depth)
            term = jnp.dot(
                rows[:, k * depth:(k + 1) * depth],
                w_down[0, pl.ds(d, depth), c:c + step],
                preferred_element_type=jnp.float32,
            )
            total = term if total is None else total + term
        if not last:
            outs[0][:, c:c + step] = total
            continue
        total = total.astype(jnp.bfloat16)
        for e in range(experts):
            outs[e][:, c:c + step] = total[e * each:(e + 1) * each, :]


def share_kernel(experts, groups, count, chosen, cap, width, *refs):
    blocks, outs = refs[:groups], refs[groups:]
    each = groups * cap
    tokens = groups * count
    ep, sub = lax.axis_index("ep"), lax.axis_index("sub")
    meta = jnp.concatenate([b[:, width:width + LANES].astype(jnp.float32) for b in blocks], axis=0)
    a, b = iota((tokens, tokens), 0), iota((tokens, tokens), 1)
    earlier = as_bf16((a // count == b // count) & (b < a))
    lane = iota((tokens, LANES), 1)
    token, slot = iota((tokens, each), 0), iota((tokens, each), 1)
    mine = slot // cap == (token // count) ^ sub
    place = (slot % cap).astype(jnp.float32)
    weights = [[] for _ in range(PIECES)]
    for e in range(experts):
        named = ((lane < chosen) & (meta == (ep ^ e).astype(jnp.float32))).astype(jnp.float32)
        present = jnp.broadcast_to(jnp.max(named, axis=1, keepdims=True), (tokens, each))
        rank = jnp.dot(earlier, present.astype(jnp.bfloat16), preferred_element_type=jnp.float32)
        taken = mine & (place == rank) & (present > 0.5)
        for p in range(PIECES):
            share = 0.0
            for k in range(chosen):
                at = (p + 1) * chosen + k
                share = share + meta[:, at:at + 1] * named[:, k:k + 1]
            weights[p].append(jnp.where(taken, share, 0.0))
    for p in range(PIECES):
        outs[p][...] = jnp.concatenate(weights[p], axis=1).astype(jnp.bfloat16)


def combine_kernel(experts, groups, count, *refs):
    weights, got = refs[:PIECES], refs[PIECES:PIECES + experts]
    outs, rows = refs[PIECES + experts:-1], refs[-1]
    each = got[0].shape[0]
    for e in range(experts):
        rows[e * each:(e + 1) * each, :] = got[e][...]
    total = 0.0
    for w in weights[::-1]:
        total = total + jnp.dot(w[...], rows[...], preferred_element_type=jnp.float32)
    total = total.astype(jnp.bfloat16)
    for k in range(groups):
        outs[k][...] = total[k * count:(k + 1) * count, :]


def place_kernel(*refs):
    parts, out, sems = refs[:-2][::-1], refs[-2], refs[-1]
    columns = parts[0].shape[1]
    sub = lax.axis_index("sub")
    moves = []
    for k, part in enumerate(parts):
        at = pl.multiple_of((sub ^ k) * columns, columns)
        moves.append(pltpu.make_async_copy(part, out.at[:, pl.ds(at, columns)], sems.at[k]))
    for move in moves:
        move.start()
    for move in moves:
        move.wait()


def body(tokens, routes, gates, gate_weight, up_weight, down_weight):
    experts = lax.axis_size("ep")
    groups = lax.axis_size("sub")
    count, width = tokens.shape
    chosen = routes.shape[1]
    cap = count * chosen * 9 // (8 * experts)
    devices = experts * groups
    chunk = min(16, devices)

    def array(*shape):
        return jax.ShapeDtypeStruct(shape, jnp.bfloat16)

    def limit(mib):
        return pltpu.CompilerParams(vmem_limit_bytes=mib << 20)

    own = pl.pallas_call(
        pack_kernel,
        out_shape=array(count, width + LANES),
        in_specs=[HBM] * 3,
        out_specs=VMEM,
        scratch_shapes=[
            pltpu.VMEM((chosen, count), jnp.int32),
            pltpu.VMEM((chosen, count), jnp.float32),
            pltpu.SemaphoreType.DMA((3,)),
        ],
        compiler_params=pltpu.CompilerParams(vmem_limit_bytes=67_000_000),
        name="pack",
    )(tokens, routes.T, gates.T)

    def hold(x):
        return pl.pallas_call(
            hold_kernel,
            out_shape=array(*x.shape),
            in_specs=[VMEM],
            out_specs=VMEM,
            cost_estimate=pl.CostEstimate(flops=3000000000, bytes_accessed=0, transcendentals=0),
            compiler_params=limit(1),
            name="hold",
        )(x)

    got = {(0, 0): own}
    single = [1 << b for b in range(groups.bit_length() - 1)]
    far = range(2, experts, 2)
    for kz in single[::-1]:
        got[kz, 0] = swap(own, "sub", groups, kz)
    for ky in far:
        got[0, ky] = swap(own, "ep", experts, ky)
    got[0, 2] = hold(got[0, 2])
    got[1, 0] = hold(got[1, 0])
    relayed = [kz for kz in range(1, groups) if kz not in single]
    for kz in relayed:
        for ky in far:
            got[kz, ky] = swap(got[0, ky], "sub", groups, kz)
    for kz in relayed:
        low = kz & -kz
        got[kz, 0] = swap(got[kz ^ low, 0], "sub", groups, low)
    for kz in single:
        for ky in far:
            got[kz, ky] = swap(got[kz, 0], "ep", experts, ky)
    later = {(0, 0): (1, 2), (1, 0): (1, 2), (2, 0): (1, 2), (0, 2): (1, 2)}
    for kz in range(groups):
        for ky in range(0, experts, 2):
            block = got[kz, ky]
            if (kz, ky) in later:
                block = lax.optimization_barrier((block, got[later[kz, ky]]))[0]
            got[kz, ky + 1] = swap(block, "ep", experts, 1)
    arrays = [got[kz, ke] for ke in range(experts) for kz in range(groups)][::-1]

    columns = gate_weight.shape[2]
    hidden = pl.pallas_call(
        functools.partial(up_kernel, len(arrays), count, chosen, cap, chunk, width),
        out_shape=array(devices * cap, columns),
        in_specs=[VMEM] * (len(arrays) + 2),
        out_specs=VMEM,
        scratch_shapes=[
            pltpu.VMEM((devices * count, width + LANES), jnp.bfloat16),
            pltpu.VMEM((devices * cap, columns), jnp.float32),
        ],
        compiler_params=limit(12 if devices <= 16 else 24),
        name="gate_up",
    )(*arrays, gate_weight, up_weight)

    parts = [hidden] + [swap(hidden, "sub", groups, k) for k in range(1, groups)]
    shares = pl.pallas_call(
        functools.partial(share_kernel, experts, groups, count, chosen, cap, width),
        out_shape=[array(groups * count, devices * cap)] * PIECES,
        in_specs=[VMEM] * groups,
        out_specs=[VMEM] * PIECES,
        compiler_params=limit(8 if devices <= 16 else 24),
        name="shares",
    )(*[got[k, 0] for k in range(groups)])
    out_cols = down_weight.shape[2]

    def down(first, n, *more):
        last = first + n == groups
        out = [array(groups * cap, out_cols)] * experts
        if not last:
            out = [jax.ShapeDtypeStruct((devices * cap, out_cols), jnp.float32)]
        return pl.pallas_call(
            functools.partial(down_kernel, experts, first, n, last),
            out_shape=out,
            in_specs=[VMEM] * (n + 1 + (first > 0)),
            out_specs=[VMEM] * len(out),
            scratch_shapes=[pltpu.VMEM((devices * cap, n * columns), jnp.bfloat16)],
            compiler_params=limit(8 if devices <= 16 else 24),
            name=f"down_{first}",
        )(*(parts[first:first + n][::-1] if first else more), down_weight, *(more if first else ()))

    own_part, *shares = lax.optimization_barrier([parts[0]] + list(shares))
    sent = down(1, groups - 1, *down(0, 1, own_part))

    came = [sent[0]] + [swap(sent[e], "ep", experts, e) for e in range(1, experts)]
    summed = pl.pallas_call(
        functools.partial(combine_kernel, experts, groups, count),
        out_shape=[array(count, out_cols)] * groups,
        in_specs=[VMEM] * (PIECES + experts),
        out_specs=[VMEM] * groups,
        scratch_shapes=[pltpu.VMEM((devices * cap, out_cols), jnp.bfloat16)],
        compiler_params=limit(8 if devices <= 16 else 24),
        name="combine",
    )(*shares, *came)

    home = [summed[0]] + [swap(summed[k], "sub", groups, k) for k in range(1, groups)]
    return pl.pallas_call(
        place_kernel,
        out_shape=array(count, width),
        in_specs=[VMEM] * groups,
        out_specs=HBM,
        scratch_shapes=[pltpu.SemaphoreType.DMA((groups,))],
        compiler_params=limit(1),
        name="place",
    )(*home[::-1])


def solution(mesh):
    return jax.shard_map(
        body,
        mesh=mesh,
        in_specs=(
            P(("groups", "ep", "sub"), None),
            P(("groups", "ep", "sub"), None),
            P(("groups", "ep", "sub"), None),
            P("ep", None, "sub"),
            P("ep", None, "sub"),
            P("ep", None, "sub"),
        ),
        out_specs=P(("groups", "ep", "sub"), None),
        check_vma=False,
    )
```

```python
import functools

import jax
import jax.numpy as jnp
from jax import lax
from jax.experimental import pallas as pl
from jax.experimental.pallas import tpu as pltpu
from jax.sharding import PartitionSpec as P

LANES = 128
PIECES = 3
VMEM = pl.BlockSpec(memory_space=pltpu.VMEM)
HBM = pl.BlockSpec(memory_space=pltpu.HBM)


def iota(shape, dim):
    return lax.broadcasted_iota(jnp.int32, shape, dim)


def as_bf16(mask):
    return mask.astype(jnp.float32).astype(jnp.bfloat16)


def swap(x, axis, size, k):
    return lax.ppermute(x, axis, [(i, i ^ k) for i in range(size)])


def pack_kernel(tokens, routes, gates, out, named, shares, sems):
    count, width = tokens.shape
    chosen = routes.shape[0]
    moves = [
        pltpu.make_async_copy(routes, named, sems.at[0]),
        pltpu.make_async_copy(gates, shares, sems.at[1]),
        pltpu.make_async_copy(tokens, out.at[:, pl.ds(0, width)], sems.at[2]),
    ]
    for move in moves[:3]:
        move.start()
    for move in moves[:2]:
        move.wait()
    diagonal = iota((count, count), 0) == iota((count, count), 1)
    lane = iota((count, LANES), 1)
    me = lax.axis_index("ep") * lax.axis_size("sub") + lax.axis_index("sub")
    owner = (PIECES + 1) * chosen
    meta = jnp.where(lane == owner, me.astype(jnp.float32), jnp.zeros((count, LANES), jnp.float32))
    for k in range(chosen):
        columns = [named[k:k + 1, :].astype(jnp.float32)]
        rest = shares[k:k + 1, :]
        for _ in range(PIECES):
            piece = rest.astype(jnp.bfloat16).astype(jnp.float32)
            columns.append(piece)
            rest = rest - piece
        for p, value in enumerate(columns):
            value = jnp.where(diagonal, jnp.broadcast_to(value, (count, count)), 0.0)
            meta = jnp.where(lane == p * chosen + k, jnp.sum(value, axis=1, keepdims=True), meta)
    out[:, width:] = meta.astype(jnp.bfloat16)
    moves[2].wait()


def gather_rows(arrays, xs):
    at, held = 0, None
    for ref in arrays:
        rows = ref.shape[0]
        if rows % 16 == 0:
            xs[at:at + rows, :] = ref[...]
            at += rows
        elif held is None:
            held = ref
        else:
            xs[at:at + 2 * rows, :] = jnp.concatenate([held[...], ref[...]], axis=0)
            at, held = at + 2 * rows, None


def hold_kernel(x, out):
    out[...] = x[...]


def up_kernel(n, count, chosen, cap, chunk, width, *refs):
    arrays, (w_gate, w_up, out, xs, total) = refs[:n], refs[n:]
    columns = out.shape[1]
    slots = out.shape[0]
    rows = count * chunk
    parts = xs.shape[0] // rows
    expert = lax.axis_index("ep")
    gather_rows(arrays, xs)
    step = min(256, columns)

    def part(j, carry):
        at = pl.multiple_of(j * rows, rows)
        meta = jnp.transpose(xs[pl.ds(at, rows), width:width + LANES].astype(jnp.float32))
        named = (iota((LANES, rows), 0) < chosen) & (meta == expert.astype(jnp.float32))
        present = jnp.max(named.astype(jnp.float32), axis=0, keepdims=True)
        a, b = iota((rows, rows), 0), iota((rows, rows), 1)
        earlier = as_bf16((a // count == b // count) & (a < b))
        many = jnp.broadcast_to(present, (slots, rows))
        rank = jnp.dot(many.astype(jnp.bfloat16), earlier, preferred_element_type=jnp.float32)
        slot = iota((slots, rows), 0)
        lane = (PIECES + 1) * chosen
        mine = (slot // cap).astype(jnp.float32) == meta[lane:lane + 1, :]
        pick = as_bf16(mine & ((slot % cap).astype(jnp.float32) == rank) & (many > 0.5))
        for c in range(0, columns, step):
            x = xs[pl.ds(at, rows), :width]
            gate = jnp.dot(x, w_gate[0, :, c:c + step], preferred_element_type=jnp.float32)
            up = jnp.dot(x, w_up[0, :, c:c + step], preferred_element_type=jnp.float32)
            hidden = (gate / (1.0 + jnp.exp(-gate)) * up).astype(jnp.bfloat16)
            picked = jnp.dot(pick, hidden, preferred_element_type=jnp.float32)
            if parts == 1:
                out[:, c:c + step] = picked.astype(jnp.bfloat16)
            else:
                total[:, c:c + step] += picked
        return carry

    if parts == 1:
        part(0, 0)
    else:
        total[...] = jnp.zeros_like(total)
        lax.fori_loop(0, parts, part, 0)
        out[...] = total[...].astype(jnp.bfloat16)


def down_kernel(experts, which, last, *refs):
    n = len(which)
    parts, w_down = refs[:n], refs[n]
    before = None if which[0] == 0 else refs[n + 1]
    outs, rows = refs[n + 1 + (which[0] > 0):-1], refs[-1]
    count, depth = parts[0].shape
    columns = w_down.shape[2]
    each = count // experts
    ep, sub = lax.axis_index("ep"), lax.axis_index("sub")
    for e in range(experts):
        at = pl.multiple_of((ep ^ e) * each, each)
        for k in range(n):
            rows[e * each:(e + 1) * each, k * depth:(k + 1) * depth] = parts[k][pl.ds(at, each), :]
    step = 256 if columns % 256 == 0 else 128
    for c in range(0, columns, step):
        total = None if before is None else before[:, c:c + step]
        for k in range(n):
            d = pl.multiple_of((sub ^ which[k]) * depth, depth)
            term = jnp.dot(
                rows[:, k * depth:(k + 1) * depth],
                w_down[0, pl.ds(d, depth), c:c + step],
                preferred_element_type=jnp.float32,
            )
            total = term if total is None else total + term
        if not last:
            outs[0][:, c:c + step] = total
            continue
        total = total.astype(jnp.bfloat16)
        for e in range(experts):
            outs[e][:, c:c + step] = total[e * each:(e + 1) * each, :]


def share_kernel(experts, groups, count, chosen, cap, width, *refs):
    blocks, outs = refs[:groups], refs[groups:]
    each = groups * cap
    tokens = groups * count
    ep, sub = lax.axis_index("ep"), lax.axis_index("sub")
    meta = jnp.concatenate([b[:, width:width + LANES].astype(jnp.float32) for b in blocks], axis=0)
    a, b = iota((tokens, tokens), 0), iota((tokens, tokens), 1)
    earlier = as_bf16((a // count == b // count) & (b < a))
    lane = iota((tokens, LANES), 1)
    token, slot = iota((tokens, each), 0), iota((tokens, each), 1)
    mine = slot // cap == (token // count) ^ sub
    place = (slot % cap).astype(jnp.float32)
    weights = [[] for _ in range(PIECES)]
    for e in range(experts):
        named = ((lane < chosen) & (meta == (ep ^ e).astype(jnp.float32))).astype(jnp.float32)
        present = jnp.broadcast_to(jnp.max(named, axis=1, keepdims=True), (tokens, each))
        rank = jnp.dot(earlier, present.astype(jnp.bfloat16), preferred_element_type=jnp.float32)
        taken = mine & (place == rank) & (present > 0.5)
        for p in range(PIECES):
            share = 0.0
            for k in range(chosen):
                at = (p + 1) * chosen + k
                share = share + meta[:, at:at + 1] * named[:, k:k + 1]
            weights[p].append(jnp.where(taken, share, 0.0))
    for p in range(PIECES):
        outs[p][...] = jnp.concatenate(weights[p], axis=1).astype(jnp.bfloat16)


def combine_kernel(experts, groups, count, *refs):
    weights, got = refs[:PIECES], refs[PIECES:PIECES + experts]
    outs, rows = refs[PIECES + experts:-1], refs[-1]
    each = got[0].shape[0]
    for e in range(experts):
        rows[e * each:(e + 1) * each, :] = got[e][...]
    total = 0.0
    for w in weights[::-1]:
        total = total + jnp.dot(w[...], rows[...], preferred_element_type=jnp.float32)
    total = total.astype(jnp.bfloat16)
    for k in range(groups):
        outs[k][...] = total[k * count:(k + 1) * count, :]


def place_kernel(*refs):
    parts, out, sems = refs[:-2][::-1], refs[-2], refs[-1]
    columns = parts[0].shape[1]
    sub = lax.axis_index("sub")
    moves = []
    for k, part in enumerate(parts):
        at = pl.multiple_of((sub ^ k) * columns, columns)
        moves.append(pltpu.make_async_copy(part, out.at[:, pl.ds(at, columns)], sems.at[k]))
    for move in moves:
        move.start()
    for move in moves:
        move.wait()


def body(tokens, routes, gates, gate_weight, up_weight, down_weight):
    experts = lax.axis_size("ep")
    groups = lax.axis_size("sub")
    count, width = tokens.shape
    chosen = routes.shape[1]
    cap = count * chosen * 9 // (8 * experts)
    devices = experts * groups
    chunk = min(16, devices)

    def array(*shape):
        return jax.ShapeDtypeStruct(shape, jnp.bfloat16)

    def limit(mib):
        return pltpu.CompilerParams(vmem_limit_bytes=mib << 20)

    own = pl.pallas_call(
        pack_kernel,
        out_shape=array(count, width + LANES),
        in_specs=[HBM] * 3,
        out_specs=VMEM,
        scratch_shapes=[
            pltpu.VMEM((chosen, count), jnp.int32),
            pltpu.VMEM((chosen, count), jnp.float32),
            pltpu.SemaphoreType.DMA((3,)),
        ],
        compiler_params=pltpu.CompilerParams(vmem_limit_bytes=67_000_000),
        name="pack",
    )(tokens, routes.T, gates.T)

    def hold(x):
        return pl.pallas_call(
            hold_kernel,
            out_shape=array(*x.shape),
            in_specs=[VMEM],
            out_specs=VMEM,
            cost_estimate=pl.CostEstimate(flops=3000000000, bytes_accessed=0, transcendentals=0),
            compiler_params=limit(1),
            name="hold",
        )(x)

    got = {(0, 0): own}
    single = [1 << b for b in range(groups.bit_length() - 1)]
    far = range(2, experts, 2)
    for kz in single[::-1]:
        got[kz, 0] = swap(own, "sub", groups, kz)
    for ky in far:
        got[0, ky] = swap(own, "ep", experts, ky)
    got[0, 2] = hold(got[0, 2])
    got[1, 0] = hold(got[1, 0])
    relayed = [kz for kz in range(1, groups) if kz not in single]
    for kz in relayed:
        for ky in far:
            got[kz, ky] = swap(got[0, ky], "sub", groups, kz)
    for kz in relayed:
        low = kz & -kz
        got[kz, 0] = swap(got[kz ^ low, 0], "sub", groups, low)
    for kz in single:
        for ky in far:
            got[kz, ky] = swap(got[kz, 0], "ep", experts, ky)
    later = {(0, 0): (1, 2), (1, 0): (1, 2), (2, 0): (1, 2), (0, 2): (1, 2)}
    for kz in range(groups):
        for ky in range(0, experts, 2):
            block = got[kz, ky]
            if (kz, ky) in later:
                block = lax.optimization_barrier((block, got[later[kz, ky]]))[0]
            got[kz, ky + 1] = swap(block, "ep", experts, 1)
    arrays = [got[kz, ke] for ke in range(experts) for kz in range(groups)][::-1]

    columns = gate_weight.shape[2]
    hidden = pl.pallas_call(
        functools.partial(up_kernel, len(arrays), count, chosen, cap, chunk, width),
        out_shape=array(devices * cap, columns),
        in_specs=[VMEM] * (len(arrays) + 2),
        out_specs=VMEM,
        scratch_shapes=[
            pltpu.VMEM((devices * count, width + LANES), jnp.bfloat16),
            pltpu.VMEM((devices * cap, columns), jnp.float32),
        ],
        compiler_params=limit(12 if devices <= 16 else 24),
        name="gate_up",
    )(*arrays, gate_weight, up_weight)

    parts = [hidden] + [swap(hidden, "sub", groups, k) for k in range(1, groups)]
    shares = pl.pallas_call(
        functools.partial(share_kernel, experts, groups, count, chosen, cap, width),
        out_shape=[array(groups * count, devices * cap)] * PIECES,
        in_specs=[VMEM] * groups,
        out_specs=[VMEM] * PIECES,
        compiler_params=limit(8 if devices <= 16 else 24),
        name="shares",
    )(*[got[k, 0] for k in range(groups)])
    out_cols = down_weight.shape[2]

    def down(which, last, *before):
        out = [array(groups * cap, out_cols)] * experts
        if not last:
            out = [jax.ShapeDtypeStruct((devices * cap, out_cols), jnp.float32)]
        return pl.pallas_call(
            functools.partial(down_kernel, experts, which, last),
            out_shape=out,
            in_specs=[VMEM] * (len(which) + 1 + len(before)),
            out_specs=[VMEM] * len(out),
            scratch_shapes=[pltpu.VMEM((devices * cap, len(which) * columns), jnp.bfloat16)],
            compiler_params=limit(8 if devices <= 16 else 24),
            name=f"down_{which[0]}",
        )(*[parts[k] for k in which], down_weight, *before)

    parts[0], *shares = lax.optimization_barrier([parts[0]] + list(shares))
    total = down((0,), False)
    total = down((groups - 1, 1), False, *total)
    sent = down(tuple(range(groups - 2, 1, -1)), True, *total)

    came = [sent[0]] + [swap(sent[e], "ep", experts, e) for e in range(1, experts)]
    summed = pl.pallas_call(
        functools.partial(combine_kernel, experts, groups, count),
        out_shape=[array(count, out_cols)] * groups,
        in_specs=[VMEM] * (PIECES + experts),
        out_specs=[VMEM] * groups,
        scratch_shapes=[pltpu.VMEM((devices * cap, out_cols), jnp.bfloat16)],
        compiler_params=limit(8 if devices <= 16 else 24),
        name="combine",
    )(*shares, *came)

    home = [summed[0]] + [swap(summed[k], "sub", groups, k) for k in range(1, groups)]
    return pl.pallas_call(
        place_kernel,
        out_shape=array(count, width),
        in_specs=[VMEM] * groups,
        out_specs=HBM,
        scratch_shapes=[pltpu.SemaphoreType.DMA((groups,))],
        compiler_params=limit(1),
        name="place",
    )(*home[::-1])


def solution(mesh):
    return jax.shard_map(
        body,
        mesh=mesh,
        in_specs=(
            P(("groups", "ep", "sub"), None),
            P(("groups", "ep", "sub"), None),
            P(("groups", "ep", "sub"), None),
            P("ep", None, "sub"),
            P("ep", None, "sub"),
            P("ep", None, "sub"),
        ),
        out_specs=P(("groups", "ep", "sub"), None),
        check_vma=False,
    )
```

```python
import functools

import jax
import jax.numpy as jnp
from jax import lax
from jax.experimental import pallas as pl
from jax.experimental.pallas import tpu as pltpu
from jax.sharding import PartitionSpec as P

LANES = 128
PIECES = 3
VMEM = pl.BlockSpec(memory_space=pltpu.VMEM)
HBM = pl.BlockSpec(memory_space=pltpu.HBM)


def iota(shape, dim):
    return lax.broadcasted_iota(jnp.int32, shape, dim)


def as_bf16(mask):
    return mask.astype(jnp.float32).astype(jnp.bfloat16)


def swap(x, axis, size, k):
    return lax.ppermute(x, axis, [(i, i ^ k) for i in range(size)])


def pack_kernel(tokens, routes, gates, out, named, shares, sems):
    count, width = tokens.shape
    chosen = routes.shape[0]
    moves = [
        pltpu.make_async_copy(routes, named, sems.at[0]),
        pltpu.make_async_copy(gates, shares, sems.at[1]),
        pltpu.make_async_copy(tokens, out.at[:, pl.ds(0, width)], sems.at[2]),
    ]
    for move in moves[:3]:
        move.start()
    for move in moves[:2]:
        move.wait()
    diagonal = iota((count, count), 0) == iota((count, count), 1)
    lane = iota((count, LANES), 1)
    me = lax.axis_index("ep") * lax.axis_size("sub") + lax.axis_index("sub")
    owner = (PIECES + 1) * chosen
    meta = jnp.where(lane == owner, me.astype(jnp.float32), jnp.zeros((count, LANES), jnp.float32))
    for k in range(chosen):
        columns = [named[k:k + 1, :].astype(jnp.float32)]
        rest = shares[k:k + 1, :]
        for _ in range(PIECES):
            piece = rest.astype(jnp.bfloat16).astype(jnp.float32)
            columns.append(piece)
            rest = rest - piece
        for p, value in enumerate(columns):
            value = jnp.where(diagonal, jnp.broadcast_to(value, (count, count)), 0.0)
            meta = jnp.where(lane == p * chosen + k, jnp.sum(value, axis=1, keepdims=True), meta)
    out[:, width:] = meta.astype(jnp.bfloat16)
    moves[2].wait()


def gather_rows(arrays, xs):
    at, held = 0, None
    for ref in arrays:
        rows = ref.shape[0]
        if rows % 16 == 0:
            xs[at:at + rows, :] = ref[...]
            at += rows
        elif held is None:
            held = ref
        else:
            xs[at:at + 2 * rows, :] = jnp.concatenate([held[...], ref[...]], axis=0)
            at, held = at + 2 * rows, None


def hold_kernel(x, out):
    out[...] = x[...]


def up_kernel(n, count, chosen, cap, chunk, width, *refs):
    arrays, (w_gate, w_up, out, xs, total) = refs[:n], refs[n:]
    columns = out.shape[1]
    slots = out.shape[0]
    rows = count * chunk
    parts = xs.shape[0] // rows
    expert = lax.axis_index("ep")
    gather_rows(arrays, xs)
    step = columns

    def part(j, carry):
        at = pl.multiple_of(j * rows, rows)
        meta = jnp.transpose(xs[pl.ds(at, rows), width:width + LANES].astype(jnp.float32))
        named = (iota((LANES, rows), 0) < chosen) & (meta == expert.astype(jnp.float32))
        present = jnp.max(named.astype(jnp.float32), axis=0, keepdims=True)
        a, b = iota((rows, rows), 0), iota((rows, rows), 1)
        earlier = as_bf16((a // count == b // count) & (a < b))
        many = jnp.broadcast_to(present, (slots, rows))
        rank = jnp.dot(many.astype(jnp.bfloat16), earlier, preferred_element_type=jnp.float32)
        slot = iota((slots, rows), 0)
        lane = (PIECES + 1) * chosen
        mine = (slot // cap).astype(jnp.float32) == meta[lane:lane + 1, :]
        pick = as_bf16(mine & ((slot % cap).astype(jnp.float32) == rank) & (many > 0.5))
        for c in range(0, columns, step):
            x = xs[pl.ds(at, rows), :width]
            gate = jnp.dot(x, w_gate[0, :, c:c + step], preferred_element_type=jnp.float32)
            up = jnp.dot(x, w_up[0, :, c:c + step], preferred_element_type=jnp.float32)
            hidden = (gate / (1.0 + jnp.exp(-gate)) * up).astype(jnp.bfloat16)
            picked = jnp.dot(pick, hidden, preferred_element_type=jnp.float32)
            if parts == 1:
                out[:, c:c + step] = picked.astype(jnp.bfloat16)
            else:
                total[:, c:c + step] += picked
        return carry

    if parts == 1:
        part(0, 0)
    else:
        total[...] = jnp.zeros_like(total)
        lax.fori_loop(0, parts, part, 0)
        out[...] = total[...].astype(jnp.bfloat16)


def down_kernel(experts, which, last, *refs):
    n = len(which)
    parts, w_down = refs[:n], refs[n]
    before = None if which[0] == 0 else refs[n + 1]
    outs, rows = refs[n + 1 + (which[0] > 0):-1], refs[-1]
    count, depth = parts[0].shape
    columns = w_down.shape[2]
    each = count // experts
    ep, sub = lax.axis_index("ep"), lax.axis_index("sub")
    for e in range(experts):
        at = pl.multiple_of((ep ^ e) * each, each)
        for k in range(n):
            rows[e * each:(e + 1) * each, k * depth:(k + 1) * depth] = parts[k][pl.ds(at, each), :]
    step = 256 if columns % 256 == 0 else 128
    for c in range(0, columns, step):
        total = None if before is None else before[:, c:c + step]
        for k in range(n):
            d = pl.multiple_of((sub ^ which[k]) * depth, depth)
            term = jnp.dot(
                rows[:, k * depth:(k + 1) * depth],
                w_down[0, pl.ds(d, depth), c:c + step],
                preferred_element_type=jnp.float32,
            )
            total = term if total is None else total + term
        if not last:
            outs[0][:, c:c + step] = total
            continue
        total = total.astype(jnp.bfloat16)
        for e in range(experts):
            outs[e][:, c:c + step] = total[e * each:(e + 1) * each, :]


def share_kernel(experts, groups, count, chosen, cap, width, *refs):
    blocks, outs = refs[:groups], refs[groups:]
    each = groups * cap
    tokens = groups * count
    ep, sub = lax.axis_index("ep"), lax.axis_index("sub")
    meta = jnp.concatenate([b[:, width:width + LANES].astype(jnp.float32) for b in blocks], axis=0)
    a, b = iota((tokens, tokens), 0), iota((tokens, tokens), 1)
    earlier = as_bf16((a // count == b // count) & (b < a))
    lane = iota((tokens, LANES), 1)
    token, slot = iota((tokens, each), 0), iota((tokens, each), 1)
    mine = slot // cap == (token // count) ^ sub
    place = (slot % cap).astype(jnp.float32)
    weights = [[] for _ in range(PIECES)]
    for e in range(experts):
        named = ((lane < chosen) & (meta == (ep ^ e).astype(jnp.float32))).astype(jnp.float32)
        present = jnp.broadcast_to(jnp.max(named, axis=1, keepdims=True), (tokens, each))
        rank = jnp.dot(earlier, present.astype(jnp.bfloat16), preferred_element_type=jnp.float32)
        taken = mine & (place == rank) & (present > 0.5)
        for p in range(PIECES):
            share = 0.0
            for k in range(chosen):
                at = (p + 1) * chosen + k
                share = share + meta[:, at:at + 1] * named[:, k:k + 1]
            weights[p].append(jnp.where(taken, share, 0.0))
    for p in range(PIECES):
        outs[p][...] = jnp.concatenate(weights[p], axis=1).astype(jnp.bfloat16)


def combine_kernel(experts, groups, count, *refs):
    weights, got = refs[:PIECES], refs[PIECES:PIECES + experts]
    outs, rows = refs[PIECES + experts:-1], refs[-1]
    each = got[0].shape[0]
    for e in range(experts):
        rows[e * each:(e + 1) * each, :] = got[e][...]
    tall = jnp.concatenate([w[...] for w in weights[::-1]], axis=0)
    terms = jnp.dot(tall, rows[...], preferred_element_type=jnp.float32)
    tokens = weights[0].shape[0]
    total = 0.0
    for p in range(PIECES):
        total = total + terms[p * tokens:(p + 1) * tokens]
    total = total.astype(jnp.bfloat16)
    for k in range(groups):
        outs[k][...] = total[k * count:(k + 1) * count, :]


def place_kernel(*refs):
    parts, out, sems = refs[:-2][::-1], refs[-2], refs[-1]
    columns = parts[0].shape[1]
    sub = lax.axis_index("sub")
    moves = []
    for k, part in enumerate(parts):
        at = pl.multiple_of((sub ^ k) * columns, columns)
        moves.append(pltpu.make_async_copy(part, out.at[:, pl.ds(at, columns)], sems.at[k]))
    for move in moves:
        move.start()
    for move in moves:
        move.wait()


def body(tokens, routes, gates, gate_weight, up_weight, down_weight):
    experts = lax.axis_size("ep")
    groups = lax.axis_size("sub")
    count, width = tokens.shape
    chosen = routes.shape[1]
    cap = count * chosen * 9 // (8 * experts)
    devices = experts * groups
    chunk = min(16, devices)

    def array(*shape):
        return jax.ShapeDtypeStruct(shape, jnp.bfloat16)

    def limit(mib):
        return pltpu.CompilerParams(vmem_limit_bytes=mib << 20)

    own = pl.pallas_call(
        pack_kernel,
        out_shape=array(count, width + LANES),
        in_specs=[HBM] * 3,
        out_specs=VMEM,
        scratch_shapes=[
            pltpu.VMEM((chosen, count), jnp.int32),
            pltpu.VMEM((chosen, count), jnp.float32),
            pltpu.SemaphoreType.DMA((3,)),
        ],
        compiler_params=pltpu.CompilerParams(vmem_limit_bytes=67_000_000),
        name="pack",
    )(tokens, routes.T, gates.T)

    def hold(x):
        return pl.pallas_call(
            hold_kernel,
            out_shape=array(*x.shape),
            in_specs=[VMEM],
            out_specs=VMEM,
            cost_estimate=pl.CostEstimate(flops=3000000000, bytes_accessed=0, transcendentals=0),
            compiler_params=limit(1),
            name="hold",
        )(x)

    got = {(0, 0): own}
    single = [1 << b for b in range(groups.bit_length() - 1)]
    far = range(2, experts, 2)
    for kz in single[::-1]:
        got[kz, 0] = swap(own, "sub", groups, kz)
    for ky in far:
        got[0, ky] = swap(own, "ep", experts, ky)
    got[0, 2] = hold(got[0, 2])
    got[1, 0] = hold(got[1, 0])
    relayed = [kz for kz in range(1, groups) if kz not in single]
    for kz in relayed:
        for ky in far:
            got[kz, ky] = swap(got[0, ky], "sub", groups, kz)
    for kz in relayed:
        low = kz & -kz
        got[kz, 0] = swap(got[kz ^ low, 0], "sub", groups, low)
    for kz in single:
        for ky in far:
            got[kz, ky] = swap(got[kz, 0], "ep", experts, ky)
    later = {(0, 0): (1, 2), (1, 0): (1, 2), (2, 0): (1, 2), (0, 2): (1, 2)}
    for kz in range(groups):
        for ky in range(0, experts, 2):
            block = got[kz, ky]
            if (kz, ky) in later:
                block = lax.optimization_barrier((block, got[later[kz, ky]]))[0]
            got[kz, ky + 1] = swap(block, "ep", experts, 1)
    arrays = [got[kz, ke] for ke in range(experts) for kz in range(groups)][::-1]

    columns = gate_weight.shape[2]
    hidden = pl.pallas_call(
        functools.partial(up_kernel, len(arrays), count, chosen, cap, chunk, width),
        out_shape=array(devices * cap, columns),
        in_specs=[VMEM] * (len(arrays) + 2),
        out_specs=VMEM,
        scratch_shapes=[
            pltpu.VMEM((devices * count, width + LANES), jnp.bfloat16),
            pltpu.VMEM((devices * cap, columns), jnp.float32),
        ],
        compiler_params=limit(12 if devices <= 16 else 24),
        name="gate_up",
    )(*arrays, gate_weight, up_weight)

    parts = [hidden] + [swap(hidden, "sub", groups, k) for k in range(1, groups)]
    shares = pl.pallas_call(
        functools.partial(share_kernel, experts, groups, count, chosen, cap, width),
        out_shape=[array(groups * count, devices * cap)] * PIECES,
        in_specs=[VMEM] * groups,
        out_specs=[VMEM] * PIECES,
        compiler_params=limit(8 if devices <= 16 else 24),
        name="shares",
    )(*[got[k, 0] for k in range(groups)])
    out_cols = down_weight.shape[2]

    def down(which, last, *before):
        out = [array(groups * cap, out_cols)] * experts
        if not last:
            out = [jax.ShapeDtypeStruct((devices * cap, out_cols), jnp.float32)]
        return pl.pallas_call(
            functools.partial(down_kernel, experts, which, last),
            out_shape=out,
            in_specs=[VMEM] * (len(which) + 1 + len(before)),
            out_specs=[VMEM] * len(out),
            scratch_shapes=[pltpu.VMEM((devices * cap, len(which) * columns), jnp.bfloat16)],
            compiler_params=limit(8 if devices <= 16 else 24),
            name=f"down_{which[0]}",
        )(*[parts[k] for k in which], down_weight, *before)

    parts[0], *shares = lax.optimization_barrier([parts[0]] + list(shares))
    total = down((0,), False)
    total = down((groups - 1, 1), False, *total)
    sent = down(tuple(range(groups - 2, 1, -1)), True, *total)

    came = [sent[0]] + [swap(sent[e], "ep", experts, e) for e in range(1, experts)]
    summed = pl.pallas_call(
        functools.partial(combine_kernel, experts, groups, count),
        out_shape=[array(count, out_cols)] * groups,
        in_specs=[VMEM] * (PIECES + experts),
        out_specs=[VMEM] * groups,
        scratch_shapes=[pltpu.VMEM((devices * cap, out_cols), jnp.bfloat16)],
        compiler_params=limit(8 if devices <= 16 else 24),
        name="combine",
    )(*shares, *came)

    home = [summed[0]] + [swap(summed[k], "sub", groups, k) for k in range(1, groups)]
    return pl.pallas_call(
        place_kernel,
        out_shape=array(count, width),
        in_specs=[VMEM] * groups,
        out_specs=HBM,
        scratch_shapes=[pltpu.SemaphoreType.DMA((groups,))],
        compiler_params=limit(1),
        name="place",
    )(*home[::-1])


def solution(mesh):
    return jax.shard_map(
        body,
        mesh=mesh,
        in_specs=(
            P(("groups", "ep", "sub"), None),
            P(("groups", "ep", "sub"), None),
            P(("groups", "ep", "sub"), None),
            P("ep", None, "sub"),
            P("ep", None, "sub"),
            P("ep", None, "sub"),
        ),
        out_specs=P(("groups", "ep", "sub"), None),
        check_vma=False,
    )
```

```python
import functools

import jax
import jax.numpy as jnp
from jax import lax
from jax.experimental import pallas as pl
from jax.experimental.pallas import tpu as pltpu
from jax.sharding import PartitionSpec as P

LANES = 128
PIECES = 3
VMEM = pl.BlockSpec(memory_space=pltpu.VMEM)
HBM = pl.BlockSpec(memory_space=pltpu.HBM)


def iota(shape, dim):
    return lax.broadcasted_iota(jnp.int32, shape, dim)


def as_bf16(mask):
    return mask.astype(jnp.float32).astype(jnp.bfloat16)


def swap(x, axis, size, k):
    return lax.ppermute(x, axis, [(i, i ^ k) for i in range(size)])


def pack_kernel(tokens, routes, gates, out, named, shares, sems):
    count, width = tokens.shape
    chosen = routes.shape[0]
    moves = [
        pltpu.make_async_copy(routes, named, sems.at[0]),
        pltpu.make_async_copy(gates, shares, sems.at[1]),
        pltpu.make_async_copy(tokens, out.at[:, pl.ds(0, width)], sems.at[2]),
    ]
    for move in moves[:3]:
        move.start()
    for move in moves[:2]:
        move.wait()
    diagonal = iota((count, count), 0) == iota((count, count), 1)
    lane = iota((count, LANES), 1)
    me = lax.axis_index("ep") * lax.axis_size("sub") + lax.axis_index("sub")
    owner = (PIECES + 1) * chosen
    meta = jnp.where(lane == owner, me.astype(jnp.float32), jnp.zeros((count, LANES), jnp.float32))
    for k in range(chosen):
        columns = [named[k:k + 1, :].astype(jnp.float32)]
        rest = shares[k:k + 1, :]
        for _ in range(PIECES):
            piece = rest.astype(jnp.bfloat16).astype(jnp.float32)
            columns.append(piece)
            rest = rest - piece
        for p, value in enumerate(columns):
            value = jnp.where(diagonal, jnp.broadcast_to(value, (count, count)), 0.0)
            meta = jnp.where(lane == p * chosen + k, jnp.sum(value, axis=1, keepdims=True), meta)
    out[:, width:] = meta.astype(jnp.bfloat16)
    moves[2].wait()


def gather_rows(arrays, xs):
    at, held = 0, None
    for ref in arrays:
        rows = ref.shape[0]
        if rows % 16 == 0:
            xs[at:at + rows, :] = ref[...]
            at += rows
        elif held is None:
            held = ref
        else:
            xs[at:at + 2 * rows, :] = jnp.concatenate([held[...], ref[...]], axis=0)
            at, held = at + 2 * rows, None


def hold_kernel(x, out):
    out[...] = x[...]


def up_kernel(n, count, chosen, cap, chunk, width, *refs):
    arrays, (w_gate, w_up, out, xs, total) = refs[:n], refs[n:]
    columns = out.shape[1]
    slots = out.shape[0]
    rows = count * chunk
    parts = xs.shape[0] // rows
    expert = lax.axis_index("ep")
    gather_rows(arrays, xs)
    step = columns

    def part(j, carry):
        at = pl.multiple_of(j * rows, rows)
        meta = jnp.transpose(xs[pl.ds(at, rows), width:width + LANES].astype(jnp.float32))
        named = (iota((LANES, rows), 0) < chosen) & (meta == expert.astype(jnp.float32))
        present = jnp.max(named.astype(jnp.float32), axis=0, keepdims=True)
        a, b = iota((rows, rows), 0), iota((rows, rows), 1)
        earlier = as_bf16((a // count == b // count) & (a < b))
        many = jnp.broadcast_to(present, (slots, rows))
        rank = jnp.dot(many.astype(jnp.bfloat16), earlier, preferred_element_type=jnp.float32)
        slot = iota((slots, rows), 0)
        lane = (PIECES + 1) * chosen
        mine = (slot // cap).astype(jnp.float32) == meta[lane:lane + 1, :]
        pick = as_bf16(mine & ((slot % cap).astype(jnp.float32) == rank) & (many > 0.5))
        for c in range(0, columns, step):
            x = xs[pl.ds(at, rows), :width]
            gate = jnp.dot(x, w_gate[0, :, c:c + step], preferred_element_type=jnp.float32)
            up = jnp.dot(x, w_up[0, :, c:c + step], preferred_element_type=jnp.float32)
            hidden = (gate / (1.0 + jnp.exp(-gate)) * up).astype(jnp.bfloat16)
            picked = jnp.dot(pick, hidden, preferred_element_type=jnp.float32)
            if parts == 1:
                out[:, c:c + step] = picked.astype(jnp.bfloat16)
            else:
                total[:, c:c + step] += picked
        return carry

    if parts == 1:
        part(0, 0)
    else:
        total[...] = jnp.zeros_like(total)
        lax.fori_loop(0, parts, part, 0)
        out[...] = total[...].astype(jnp.bfloat16)


def down_kernel(experts, which, last, *refs):
    n = len(which)
    parts, w_down = refs[:n], refs[n]
    before = None if which[0] == 0 else refs[n + 1]
    outs, rows = refs[n + 1 + (which[0] > 0):-1], refs[-1]
    count, depth = parts[0].shape
    columns = w_down.shape[2]
    each = count // experts
    ep, sub = lax.axis_index("ep"), lax.axis_index("sub")
    for e in range(experts):
        at = pl.multiple_of((ep ^ e) * each, each)
        for k in range(n):
            rows[e * each:(e + 1) * each, k * depth:(k + 1) * depth] = parts[k][pl.ds(at, each), :]
    step = 256 if columns % 256 == 0 else 128
    for c in range(0, columns, step):
        total = None if before is None else before[:, c:c + step]
        for k in range(n):
            d = pl.multiple_of((sub ^ which[k]) * depth, depth)
            term = jnp.dot(
                rows[:, k * depth:(k + 1) * depth],
                w_down[0, pl.ds(d, depth), c:c + step],
                preferred_element_type=jnp.float32,
            )
            total = term if total is None else total + term
        if not last:
            outs[0][:, c:c + step] = total
            continue
        total = total.astype(jnp.bfloat16)
        for e in range(experts):
            outs[e][:, c:c + step] = total[e * each:(e + 1) * each, :]


def share_kernel(experts, groups, count, chosen, cap, width, *refs):
    blocks, outs = refs[:groups], refs[groups:]
    each = groups * cap
    tokens = groups * count
    ep, sub = lax.axis_index("ep"), lax.axis_index("sub")
    meta = jnp.concatenate([b[:, width:width + LANES].astype(jnp.float32) for b in blocks], axis=0)
    a, b = iota((tokens, tokens), 0), iota((tokens, tokens), 1)
    earlier = as_bf16((a // count == b // count) & (b < a))
    lane = iota((tokens, LANES), 1)
    token, slot = iota((tokens, each), 0), iota((tokens, each), 1)
    mine = slot // cap == (token // count) ^ sub
    place = (slot % cap).astype(jnp.float32)
    weights = [[] for _ in range(PIECES)]
    for e in range(experts):
        named = ((lane < chosen) & (meta == (ep ^ e).astype(jnp.float32))).astype(jnp.float32)
        present = jnp.broadcast_to(jnp.max(named, axis=1, keepdims=True), (tokens, each))
        rank = jnp.dot(earlier, present.astype(jnp.bfloat16), preferred_element_type=jnp.float32)
        taken = mine & (place == rank) & (present > 0.5)
        for p in range(PIECES):
            share = 0.0
            for k in range(chosen):
                at = (p + 1) * chosen + k
                share = share + meta[:, at:at + 1] * named[:, k:k + 1]
            weights[p].append(jnp.where(taken, share, 0.0))
    for p in range(PIECES):
        outs[p][...] = jnp.concatenate(weights[p], axis=1).astype(jnp.bfloat16)


def combine_kernel(experts, groups, count, *refs):
    weights, got = refs[:PIECES], refs[PIECES:PIECES + experts]
    outs, rows = refs[PIECES + experts:-1], refs[-1]
    each = got[0].shape[0]
    for e in range(experts):
        rows[e * each:(e + 1) * each, :] = got[e][...]
    tall = jnp.concatenate([w[...] for w in weights[::-1]], axis=0)
    terms = jnp.dot(tall, rows[...], preferred_element_type=jnp.float32)
    tokens = weights[0].shape[0]
    total = 0.0
    for p in range(PIECES):
        total = total + terms[p * tokens:(p + 1) * tokens]
    total = total.astype(jnp.bfloat16)
    for k in range(groups):
        outs[k][...] = total[k * count:(k + 1) * count, :]


def place_kernel(*refs):
    parts, out, sems = refs[:-2][::-1], refs[-2], refs[-1]
    columns = parts[0].shape[1]
    sub = lax.axis_index("sub")
    moves = []
    for k, part in enumerate(parts):
        at = pl.multiple_of((sub ^ k) * columns, columns)
        moves.append(pltpu.make_async_copy(part, out.at[:, pl.ds(at, columns)], sems.at[k]))
    for move in moves:
        move.start()
    for move in moves:
        move.wait()


def body(tokens, routes, gates, gate_weight, up_weight, down_weight):
    experts = lax.axis_size("ep")
    groups = lax.axis_size("sub")
    count, width = tokens.shape
    chosen = routes.shape[1]
    cap = count * chosen * 9 // (8 * experts)
    devices = experts * groups
    chunk = min(16, devices)

    def array(*shape):
        return jax.ShapeDtypeStruct(shape, jnp.bfloat16)

    def limit(mib):
        return pltpu.CompilerParams(vmem_limit_bytes=mib << 20)

    own = pl.pallas_call(
        pack_kernel,
        out_shape=array(count, width + LANES),
        in_specs=[HBM] * 3,
        out_specs=VMEM,
        scratch_shapes=[
            pltpu.VMEM((chosen, count), jnp.int32),
            pltpu.VMEM((chosen, count), jnp.float32),
            pltpu.SemaphoreType.DMA((3,)),
        ],
        compiler_params=pltpu.CompilerParams(vmem_limit_bytes=67_000_000),
        name="pack",
    )(tokens, routes.T, gates.T)

    def hold(x):
        return pl.pallas_call(
            hold_kernel,
            out_shape=array(*x.shape),
            in_specs=[VMEM],
            out_specs=VMEM,
            cost_estimate=pl.CostEstimate(flops=3000000000, bytes_accessed=0, transcendentals=0),
            compiler_params=limit(1),
            name="hold",
        )(x)

    got = {(0, 0): own}
    single = [1 << b for b in range(groups.bit_length() - 1)]
    far = range(2, experts, 2)
    for kz in single[::-1]:
        got[kz, 0] = swap(own, "sub", groups, kz)
    for ky in far:
        got[0, ky] = swap(own, "ep", experts, ky)
    got[1, 0] = hold(got[1, 0])
    got[0, 2] = hold(got[0, 2])
    relayed = [kz for kz in range(1, groups) if kz not in single]
    for kz in relayed:
        for ky in far:
            got[kz, ky] = swap(got[0, ky], "sub", groups, kz)
    for kz in relayed:
        low = kz & -kz
        got[kz, 0] = swap(got[kz ^ low, 0], "sub", groups, low)
    for kz in single:
        for ky in far:
            got[kz, ky] = swap(got[kz, 0], "ep", experts, ky)
    later = {(0, 0): (1, 2), (1, 0): (1, 2), (2, 0): (1, 2), (0, 2): (1, 2)}
    for kz in range(groups):
        for ky in range(0, experts, 2):
            block = got[kz, ky]
            if (kz, ky) in later:
                block = lax.optimization_barrier((block, got[later[kz, ky]]))[0]
            got[kz, ky + 1] = swap(block, "ep", experts, 1)
    arrays = [got[kz, ke] for ke in range(experts) for kz in range(groups)][::-1]

    columns = gate_weight.shape[2]
    hidden = pl.pallas_call(
        functools.partial(up_kernel, len(arrays), count, chosen, cap, chunk, width),
        out_shape=array(devices * cap, columns),
        in_specs=[VMEM] * (len(arrays) + 2),
        out_specs=VMEM,
        scratch_shapes=[
            pltpu.VMEM((devices * count, width + LANES), jnp.bfloat16),
            pltpu.VMEM((devices * cap, columns), jnp.float32),
        ],
        compiler_params=limit(12 if devices <= 16 else 24),
        name="gate_up",
    )(*arrays, gate_weight, up_weight)

    parts = [hidden] + [swap(hidden, "sub", groups, k) for k in range(1, groups)]
    shares = pl.pallas_call(
        functools.partial(share_kernel, experts, groups, count, chosen, cap, width),
        out_shape=[array(groups * count, devices * cap)] * PIECES,
        in_specs=[VMEM] * groups,
        out_specs=[VMEM] * PIECES,
        compiler_params=limit(8 if devices <= 16 else 24),
        name="shares",
    )(*[got[k, 0] for k in range(groups)])
    out_cols = down_weight.shape[2]

    def down(which, last, *before):
        out = [array(groups * cap, out_cols)] * experts
        if not last:
            out = [jax.ShapeDtypeStruct((devices * cap, out_cols), jnp.float32)]
        return pl.pallas_call(
            functools.partial(down_kernel, experts, which, last),
            out_shape=out,
            in_specs=[VMEM] * (len(which) + 1 + len(before)),
            out_specs=[VMEM] * len(out),
            scratch_shapes=[pltpu.VMEM((devices * cap, len(which) * columns), jnp.bfloat16)],
            compiler_params=limit(8 if devices <= 16 else 24),
            name=f"down_{which[0]}",
        )(*[parts[k] for k in which], down_weight, *before)

    parts[0], *shares = lax.optimization_barrier([parts[0]] + list(shares))
    total = down((0,), False)
    total = down((groups - 1, 1), False, *total)
    sent = down(tuple(range(groups - 2, 1, -1)), True, *total)

    came = [sent[0]] + [swap(sent[e], "ep", experts, e) for e in range(1, experts)]
    summed = pl.pallas_call(
        functools.partial(combine_kernel, experts, groups, count),
        out_shape=[array(count, out_cols)] * groups,
        in_specs=[VMEM] * (PIECES + experts),
        out_specs=[VMEM] * groups,
        scratch_shapes=[pltpu.VMEM((devices * cap, out_cols), jnp.bfloat16)],
        compiler_params=limit(8 if devices <= 16 else 24),
        name="combine",
    )(*shares, *came)

    home = [summed[0]] + [swap(summed[k], "sub", groups, k) for k in range(1, groups)]
    return pl.pallas_call(
        place_kernel,
        out_shape=array(count, width),
        in_specs=[VMEM] * groups,
        out_specs=HBM,
        scratch_shapes=[pltpu.SemaphoreType.DMA((groups,))],
        compiler_params=limit(1),
        name="place",
    )(*home[::-1])


def solution(mesh):
    return jax.shard_map(
        body,
        mesh=mesh,
        in_specs=(
            P(("groups", "ep", "sub"), None),
            P(("groups", "ep", "sub"), None),
            P(("groups", "ep", "sub"), None),
            P("ep", None, "sub"),
            P("ep", None, "sub"),
            P("ep", None, "sub"),
        ),
        out_specs=P(("groups", "ep", "sub"), None),
        check_vma=False,
    )
```
